256 devices in a mesh: dp: 4 (over z_lo, core), segment: 4 (over z_hi), tensor: 16 (over x, y).
Axes of the slice: x: 4, y: 4, z: 8 (z_hi: 4, z_lo: 2; z = z_hi * 2 + z_lo), core: 2. Of those that a mesh axis runs over, the one named last changes fastest.
Arguments:
- checkpoints: bfloat16 [4, 512, 5280], P('segment', 'dp', 'tensor'), may hold values from -100 to 100
- cot_out: bfloat16 [512, 5280], P('dp', 'tensor'), may hold values from -6 to 6
- prelude_gain: float32 [5280], P('tensor'), may hold values from 0.5 to 1.5
- coda_gain: float32 [5280], P('tensor'), may hold values from 0.5 to 1.5
- mlp_gain: float32 [5280], P('dp'), may hold values from 0.5 to 1.5
- adapt_state: bfloat16 [5280, 5280], P('tensor', 'dp'), may hold values from -0.0625 to 0.0625
- adapt_inject: bfloat16 [5280, 5280], P('tensor', 'dp'), may hold values from -0.0625 to 0.0625
- mlp_gate: bfloat16 [5280, 8960], P('dp', 'tensor'), may hold values from -0.078125 to 0.078125
- mlp_up: bfloat16 [5280, 8960], P('dp', 'tensor'), may hold values from -0.078125 to 0.078125
- mlp_down: bfloat16 [8960, 5280], P('tensor', 'dp'), may hold values from -0.0625 to 0.0625
Outputs:
- grad_prelude_hidden: bfloat16 [512, 5280], P('dp', 'tensor')
- grad_prelude_gain: float32 [5280], P('tensor')
- grad_coda_gain: float32 [5280], P('tensor')
- grad_adapt_state: bfloat16 [5280, 5280], P('tensor', ('dp', 'segment'))
- grad_adapt_inject: bfloat16 [5280, 5280], P('tensor', ('dp', 'segment'))
- grad_gate: bfloat16 [5280, 8960], P(('dp', 'segment'), 'tensor')
- grad_up: bfloat16 [5280, 8960], P(('dp', 'segment'), 'tensor')
- grad_down: bfloat16 [8960, 5280], P('tensor', ('dp', 'segment'))
- grad_mlp_gain: bfloat16 [5280], P(('dp', 'segment'))
The draws below stay inside these ranges and needn't reach their ends.
All inputs are finite; a program needn't handle non-finite values.
Results may differ from the reference program's by a relative error of at most 0.035.
Values may be sent and summed in bfloat16 or wider, within the bound.
No kernel may reach another device: no remote copies, remote signals or barrier semaphores. Data moves between devices by JAX's collectives and lax.ppermute only.
A program may use at most 128 MiB of HBM per device.

```python
import math
import jax
import jax.numpy as jnp
from jax import lax

D = 5280
FF = 8960
TOKENS = 512


def draw_checkpoints(key, part):
    key = jax.random.fold_in(key, 17)
    base_key, row_key, col_key = jax.random.split(key, 3)
    full_shape = (4, TOKENS, D)
    row_factor = jnp.exp(jax.random.uniform(row_key, (4, TOKENS, 1), jnp.float32) * math.log(10.0))
    col_factor = jnp.exp(jax.random.uniform(col_key, (4, 1, D), jnp.float32) * math.log(10.0))
    base_draw = jnp.clip(jax.random.normal(base_key, full_shape, jnp.float32), -4.0, 4.0)
    return (0.25 * base_draw * row_factor * col_factor).astype(jnp.bfloat16)


def block_levels(key, shape, cuts, low, high):
    gain, own = 1.0, jax.random.fold_in(key, 6)
    for position, blocks in cuts:
        heights = jnp.exp(jax.random.uniform(jax.random.fold_in(own, position), (blocks,), jnp.float32, low / len(cuts), high / len(cuts)))
        gain = gain * jnp.repeat(heights, shape[position] // blocks).reshape([-1 if axis == position else 1 for axis in range(len(shape))])
    return gain


def bell_draw(stream_key, dims, width, reach, cuts=(), kind=jnp.bfloat16):
    array = jax.random.normal(stream_key, dims, jnp.float32) * width
    if len(cuts) > 0:
        array = block_levels(stream_key, dims, cuts, -0.22, 0.18) * array
    return jnp.clip(array, min=-reach, max=reach).astype(kind)


def setup_inputs(seed: int = 0) -> dict:
    arg_keys = jax.random.split(jax.random.key(seed), 11)
    checkpoints = draw_checkpoints(jax.random.fold_in(arg_keys[10], 71), 0)
    cot_out = bell_draw(arg_keys[1], (TOKENS, D), 1.0, 6.0, ((0, 4), (1, 16)))
    prelude_gain = jnp.clip(1.0 + 0.1 * jax.random.normal(arg_keys[2], (D,), jnp.float32), 0.5, 1.5)
    coda_gain = jnp.clip(1.0 + 0.1 * jax.random.normal(arg_keys[3], (D,), jnp.float32), 0.5, 1.5)
    mlp_gain = jnp.clip(1.0 + 0.1 * jax.random.normal(arg_keys[4], (D,), jnp.float32), 0.5, 1.5)
    adapt_state = bell_draw(arg_keys[5], (D, D), (2 * D) ** -0.5, 0.0625, ((0, 16), (1, 4)))
    adapt_inject = bell_draw(arg_keys[6], (D, D), (2 * D) ** -0.5, 0.0625, ((0, 16), (1, 4)))
    mlp_gate = bell_draw(arg_keys[7], (D, FF), D ** -0.5, 0.078125, ((0, 4), (1, 16)))
    mlp_up = bell_draw(arg_keys[8], (D, FF), D ** -0.5, 0.078125, ((0, 4), (1, 16)))
    mlp_down = bell_draw(arg_keys[9], (FF, D), FF ** -0.5, 0.0625, ((0, 16), (1, 4)))
    return {"checkpoints": checkpoints, "cot_out": cot_out, "prelude_gain": prelude_gain, "coda_gain": coda_gain, "mlp_gain": mlp_gain, "adapt_state": adapt_state, "adapt_inject": adapt_inject, "mlp_gate": mlp_gate, "mlp_up": mlp_up, "mlp_down": mlp_down}


EPSILON = 1e-06

def inverse_rms(values):
    return lax.rsqrt(lax.optimization_barrier(jnp.mean(values * values, axis=-1, keepdims=True)) + EPSILON)

def product(left, right):
    return jnp.dot(left, right, preferred_element_type=jnp.float32)

def core_backward(state, inject, cotangent, adapt_state, adapt_inject, mlp_gain, mlp_gate, mlp_up, mlp_down):
    mixed = (product(state, adapt_state) + product(inject, adapt_inject)).astype(jnp.bfloat16)
    mixed_f = mixed.astype(jnp.float32)
    mixed_scale = inverse_rms(mixed_f)
    normed = (mixed_f * mixed_scale * mlp_gain).astype(jnp.bfloat16)
    gate_value = product(normed, mlp_gate)
    up_value = product(normed, mlp_up)
    sigmoid_gate = jax.nn.sigmoid(gate_value)
    activated = gate_value * sigmoid_gate
    hidden = (activated * up_value).astype(jnp.bfloat16)
    g_hidden = product(cotangent, mlp_down.T)
    grad_down = product(hidden.T, cotangent)
    g_gate = (g_hidden * up_value * sigmoid_gate * (1.0 + gate_value * (1.0 - sigmoid_gate))).astype(jnp.bfloat16)
    g_up = (g_hidden * activated).astype(jnp.bfloat16)
    grad_gate = product(normed.T, g_gate)
    grad_up = product(normed.T, g_up)
    g_normed = product(g_gate, mlp_gate.T) + product(g_up, mlp_up.T)
    weighted = g_normed * mlp_gain
    inner = lax.optimization_barrier(jnp.mean(weighted * mixed_f, axis=-1, keepdims=True))
    g_mixed = (cotangent.astype(jnp.float32) + mixed_scale * weighted - mixed_f * mixed_scale ** 3 * inner).astype(jnp.bfloat16)
    grad_gain = lax.optimization_barrier(jnp.sum(g_normed * mixed_f * mixed_scale, axis=0))
    g_state = product(g_mixed, adapt_state.T)
    g_inject = product(g_mixed, adapt_inject.T)
    grad_as = product(state.T, g_mixed)
    grad_ai = product(inject.T, g_mixed)
    return (g_state, g_inject, (grad_as, grad_ai, grad_gate, grad_up, grad_down, grad_gain))

def round_trip(values):
    narrow = lax.optimization_barrier(values.astype(jnp.bfloat16))
    return narrow.astype(jnp.float32)

def reference(checkpoints, cot_out, prelude_gain, coda_gain, mlp_gain, adapt_state, adapt_inject, mlp_gate, mlp_up, mlp_down):
    prelude_state = checkpoints[0].astype(jnp.float32)
    prelude_scale = inverse_rms(prelude_state)
    inject = (prelude_state * prelude_scale * prelude_gain).astype(jnp.bfloat16)
    top_state = checkpoints[3].astype(jnp.float32)
    top_scale = inverse_rms(top_state)
    cotangent = cot_out.astype(jnp.float32)
    coda_scaled = cotangent * coda_gain
    coda_inner = lax.optimization_barrier(jnp.mean(coda_scaled * top_state, axis=-1, keepdims=True))
    top_cot = (top_scale * coda_scaled - top_state * top_scale ** 3 * coda_inner).astype(jnp.bfloat16)
    grad_coda_gain = lax.optimization_barrier(jnp.sum(cotangent * top_state * top_scale, axis=0))
    upper_state, upper_inject, upper_grads = core_backward(checkpoints[2], inject, top_cot, adapt_state, adapt_inject, mlp_gain, mlp_gate, mlp_up, mlp_down)
    state_cot = upper_state.astype(jnp.bfloat16)
    ignored, lower_inject, lower_grads = core_backward(checkpoints[1], inject, state_cot, adapt_state, adapt_inject, mlp_gain, mlp_gate, mlp_up, mlp_down)
    totals = [(round_trip(upper_item) + round_trip(lower_item)).astype(jnp.bfloat16) for upper_item, lower_item in zip(upper_grads, lower_grads)]
    inject_cot = upper_inject + lower_inject
    prelude_scaled = inject_cot * prelude_gain
    prelude_inner = lax.optimization_barrier(jnp.mean(prelude_scaled * prelude_state, axis=-1, keepdims=True))
    grad_prelude_hidden = (prelude_scale * prelude_scaled - prelude_state * prelude_scale ** 3 * prelude_inner).astype(jnp.bfloat16)
    grad_prelude_gain = lax.optimization_barrier(jnp.sum(inject_cot * prelude_state * prelude_scale, axis=0))
    return (grad_prelude_hidden, grad_prelude_gain, grad_coda_gain, totals[0], totals[1], totals[2], totals[3], totals[4], totals[5])
```

```python
import jax
import jax.numpy as jnp
from jax import lax
from jax.experimental import pallas as pl
from jax.experimental.pallas import tpu as pltpu
from jax.sharding import PartitionSpec as P

D = 5280
EPSILON = 1e-06
BF = jnp.bfloat16
F32 = jnp.float32
LIMIT = 24 * 1024 * 1024


def up(value):
    return -(-value // 128) * 128


def dot(left, right):
    return jnp.dot(left, right, preferred_element_type=F32)


def dot_t(left, right):
    return lax.dot_general(left, right, (((1,), (1,)), ((), ())), preferred_element_type=F32)


def turned(value):
    return value.astype(F32).T.astype(BF)


def rounded(value):
    return value.astype(BF).astype(F32)


def lanes(shape):
    return lax.broadcasted_iota(jnp.int32, shape, len(shape) - 1)


def pick(value, lane):
    return jnp.sum(jnp.where(lanes(value.shape) == lane, value, 0.0), axis=-1, keepdims=True)


def pick_whole(value, lane):
    at = lanes(value.shape)
    return jnp.sum(jnp.where((at == lane) | (at == lane + 1), value, 0.0), axis=-1, keepdims=True)


def put_parts(value, lane, scalars):
    at = lanes(value.shape)
    for number, scalar in enumerate(scalars):
        high = rounded(scalar)
        value = jnp.where(at == lane + 2 * number, high, value)
        value = jnp.where(at == lane + 2 * number + 1, scalar - high, value)
    return value


def fused(body, outs, *args):
    scalar = [arg.dtype == jnp.int32 for arg in args]

    def kernel(*refs):
        given = [ref[0] if is_scalar else ref for ref, is_scalar in zip(refs, scalar)]
        results = body(*given)
        for ref, value in zip(refs[len(args) :], results):
            if value is not None:
                if value.shape == ref.shape:
                    ref[...] = value.astype(ref.dtype)
                else:
                    ref[...] = jnp.zeros(ref.shape, ref.dtype)
                    ref[tuple(slice(0, size) for size in value.shape)] = value.astype(ref.dtype)

    specs = [
        pl.BlockSpec(memory_space=pltpu.SMEM if is_scalar else pltpu.VMEM) for is_scalar in scalar
    ]
    return pl.pallas_call(
        kernel,
        out_shape=[jax.ShapeDtypeStruct(shape, kind) for shape, kind in outs],
        in_specs=specs,
        out_specs=[pl.BlockSpec(memory_space=pltpu.VMEM) for _ in outs],
        compiler_params=pltpu.CompilerParams(vmem_limit_bytes=LIMIT),
    )(*args)


def exchange(values, axis):
    return lax.all_to_all(values, axis, 0, 0, tiled=True)


def core_swap(values):
    return lax.ppermute(values, "dp", [(0, 1), (1, 0), (2, 3), (3, 2)])


def chip_swap(values):
    return lax.ppermute(values, "dp", [(0, 2), (2, 0), (1, 3), (3, 1)])


def rotate(values, step):
    return lax.ppermute(values, "segment", [(at, (at + step) % 4) for at in range(4)])


def halves(values, core):
    count, width = values.shape
    blocks = values.reshape(2, 2, count // 4, width)
    first, second = blocks[:, 0].reshape(count // 2, width), blocks[:, 1].reshape(count // 2, width)
    return jnp.where(core == 0, first, second), jnp.where(core == 0, second, first)


def joined(mine, other, core):
    count, width = mine.shape
    first = jnp.where(core == 0, mine, other).reshape(2, 1, count // 2, width)
    second = jnp.where(core == 0, other, mine).reshape(2, 1, count // 2, width)
    return jnp.concatenate([first, second], axis=1).reshape(2 * count, width)


def gathered_blocks(values, core, chip):
    other = core_swap(values)
    two = jnp.stack([jnp.where(core == 0, values, other), jnp.where(core == 0, other, values)])
    far = chip_swap(two)
    four = jnp.stack([jnp.where(chip == 0, two, far), jnp.where(chip == 0, far, two)])
    return four.reshape((4 * values.shape[0],) + values.shape[1:])


def local(
    checkpoints,
    cot_out,
    prelude_gain,
    coda_gain,
    mlp_gain,
    adapt_state,
    adapt_inject,
    mlp_gate,
    mlp_up,
    mlp_down,
):
    dp_count = lax.axis_size("dp")
    seg_count = lax.axis_size("segment")
    tp_count = lax.axis_size("tensor")
    dp_index = lax.axis_index("dp").astype(jnp.int32)
    seg_index = lax.axis_index("segment").astype(jnp.int32)
    tp_index = lax.axis_index("tensor").astype(jnp.int32)
    core = dp_index % 2
    chip = dp_index // 2
    block = checkpoints.shape[1]
    quarter = block // seg_count
    half = 2 * quarter
    part = checkpoints.shape[2]
    unit = up(part + 8)
    hid = mlp_gate.shape[1]
    hidw = up(hid + 8)
    group = mlp_gain.shape[0] // part
    wide = group * unit
    rows = block // tp_count
    core_s, chip_s, dp_s, tp_s = (x.reshape(1) for x in (core, chip, dp_index, tp_index))

    def padded(values, axis, width):
        return jnp.pad(
            values,
            [(0, width - size) if at == axis else (0, 0) for at, size in enumerate(values.shape)],
        )

    def grouped(values, axis):
        shape = values.shape[:axis] + (group, part) + values.shape[axis + 1 :]
        values = padded(values.reshape(shape), axis + 1, unit)
        return values.reshape(shape[:axis] + (wide,) + shape[axis + 2 :])

    chunks = padded(checkpoints[0], 1, unit).reshape(seg_count, 1, quarter, unit)
    chunks = jnp.broadcast_to(chunks, (seg_count, dp_count, quarter, unit))
    sections = exchange(
        chunks.reshape(seg_count * dp_count, quarter, unit), ("segment", "dp")
    ).reshape(4, block, unit)
    cot_own = lax.dynamic_slice_in_dim(cot_out, seg_index * quarter, quarter, 0)
    cot = gathered_blocks(padded(cot_own, 1, unit), core, chip)
    pre_gain = padded(prelude_gain[None], 1, unit)
    cod_gain = padded(coda_gain[None], 1, unit)
    gain = grouped(mlp_gain[None], 1)

    def by_columns(weight):
        count, width = weight.shape
        blocks = []
        for at in range(group):
            row = lax.broadcasted_iota(jnp.int32, (width, unit), 0)
            col = lax.broadcasted_iota(jnp.int32, (width, unit), 1)
            chosen = jnp.where((row == col + at * part) & (col < part), 1.0, 0.0).astype(BF)
            blocks.append(dot(weight[...], chosen))
        return (jnp.concatenate(blocks, axis=-1),)

    def columns(weight, count):
        return fused(by_columns, [((count, wide), BF)], weight)[0]

    w_state = columns(adapt_state, unit)
    w_inject = columns(adapt_inject, unit)
    w_gate = columns(mlp_gate.T, hidw)
    w_up = columns(mlp_up.T, hidw)
    w_down = columns(mlp_down, hidw)

    def adapter(sections, cot, pre_gain, cod_gain, w_state, w_inject):
        prelude, lower, upper, top = (sections[at].astype(F32) for at in range(4))
        cot_f = cot[...].astype(F32)
        cut = (tp_count, rows, unit)
        left = jnp.concatenate([upper.reshape(cut), lower.reshape(cut)], axis=1)
        left = left.reshape(2 * block, unit).astype(BF)
        states = dot(left, w_state[...]).reshape(tp_count, 2 * rows, wide)
        prior = dot((prelude * pre_gain[...]).astype(BF), w_inject[...]).reshape(tp_count, rows, wide)
        row_sums = [
            jnp.sum(prelude * prelude, axis=-1, keepdims=True),
            jnp.sum(top * top, axis=-1, keepdims=True),
            jnp.sum(cot_f * cod_gain[...] * top, axis=-1, keepdims=True),
        ]
        sums = put_parts(jnp.zeros((block, unit), F32), 0, row_sums)
        coda = cod_gain[...]
        high = rounded(coda)
        at = lax.broadcasted_iota(jnp.int32, (rows, unit), 0)
        gains = jnp.where(at == 0, high, jnp.where(at == 1, coda - high, 0.0))
        gains = jnp.broadcast_to(gains[None], cut)
        extra = jnp.concatenate(
            [top.reshape(cut), cot_f.reshape(cut), gains, sums.reshape(cut)], axis=-1
        )
        return (jnp.concatenate([states, prior, extra], axis=1),)

    (sent,) = fused(
        adapter,
        [((tp_count, 4 * rows, wide), BF)],
        sections,
        cot,
        pre_gain,
        cod_gain,
        w_state,
        w_inject,
    )
    arrived = exchange(sent, "tensor")

    arrived, w_gate, w_up, w_down = lax.optimization_barrier((arrived, w_gate, w_up, w_down))

    def blocks_of(value):
        return jnp.concatenate(
            [value[None, :, at * unit : (at + 1) * unit] for at in range(group)], axis=0
        )

    def mix(dp, arrived, gain):
        sums = jnp.sum(arrived[...].astype(F32), axis=0)
        totals = sums[3 * rows :, 3 * unit :]
        near = [arrived[dp * group + at].astype(F32)[3 * rows :] for at in range(group)]
        top = jnp.concatenate([value[:, :unit] for value in near], axis=-1)
        cot_f = jnp.concatenate([value[:, unit : 2 * unit] for value in near], axis=-1)
        coda = jnp.concatenate(
            [value[0:1, 2 * unit : 3 * unit] + value[1:2, 2 * unit : 3 * unit] for value in near], axis=-1
        )
        pre_scale = lax.rsqrt(pick_whole(totals, 0) / D + EPSILON)
        top_scale = lax.rsqrt(pick_whole(totals, 2) / D + EPSILON)
        inner = pick_whole(totals, 4) / D
        prior = sums[2 * rows : 3 * rows]
        mixed_u = rounded(sums[:rows] + pre_scale * prior)
        mixed_l = rounded(sums[rows : 2 * rows] + pre_scale * prior)
        cot_u = rounded(
            top_scale * (cot_f * coda) - top * (top_scale * top_scale * top_scale) * inner
        )
        own = jnp.concatenate(
            [put_parts(mixed_u, part, [pre_scale, top_scale]), mixed_l, cot_u], axis=0
        )
        spread = jnp.broadcast_to(own[None], (tp_count,) + own.shape)
        ready = jnp.concatenate([mixed_u, mixed_l], axis=0) * gain[...]
        kept = jnp.concatenate([mixed_u, mixed_l, cot_u, prior], axis=0)
        return spread, kept, blocks_of(ready)

    eight = ((rows, wide), F32)
    sent, kept_8, ready_8 = fused(
        mix,
        [((tp_count, 3 * rows, wide), BF), ((4 * rows, wide), F32), ((group, 2 * rows, unit), BF)],
        dp_s,
        arrived,
        gain,
    )

    def from_segments(values):
        return [lax.dynamic_index_in_dim(values, seg_index, 0, keepdims=False)] + [
            rotate(
                lax.dynamic_index_in_dim(values, (seg_index + step) % seg_count, 0, keepdims=False), step
            )
            for step in range(1, seg_count)
        ]

    ready_8 = from_segments(ready_8)
    arrived = exchange(sent, "tensor")

    def forward_upper(core, arrived, gain, w_gate, w_up, w_down):
        mixed = arrived[:, :rows, :].astype(F32).reshape(block, wide)
        cot_u = arrived[...].astype(F32)[:, 2 * rows :].reshape(block, wide).astype(BF)
        factor = gain[...]
        squares = jnp.sum(jnp.where(factor > 0.0, mixed * mixed, 0.0), axis=-1, keepdims=True)
        ready = (mixed * factor).astype(BF)
        sums = jnp.concatenate(
            [
                put_parts(dot_t(ready, w_gate[...]), hid, [squares]),
                dot_t(ready, w_up[...]),
                dot_t(cot_u, w_down[...]),
            ],
            axis=-1,
        )
        return halves(sums, core)

    def forward_lower(core, arrived, gain, w_gate, w_up):
        every = arrived[...].astype(F32)
        mixed_u = every[:, :rows].reshape(block, wide)
        mixed = every[:, rows : 2 * rows].reshape(block, wide)
        cot_u = every[:, 2 * rows :].reshape(block, wide)
        factor = gain[...]
        squares = jnp.sum(jnp.where(factor > 0.0, mixed * mixed, 0.0), axis=-1, keepdims=True)
        ready = (mixed * factor).astype(BF)
        sums = jnp.concatenate(
            [put_parts(dot_t(ready, w_gate[...]), hid, [squares]), dot_t(ready, w_up[...])], axis=-1
        )
        mine, other = halves(sums, core)
        scales = mixed_u[:, :unit]
        at = lanes((block, 128))
        scales = jnp.where(at == 0, pick_whole(scales, part), pick_whole(scales, part + 2))
        return mine, other, cot_u, scales

    three_half = [((half, 3 * hidw), F32), ((half, 3 * hidw), BF)]
    two_half = [((half, 2 * hidw), F32), ((half, 2 * hidw), BF)]
    mine, other = fused(forward_upper, three_half, core_s, arrived, gain, w_gate, w_up, w_down)

    def add_squares(mine, other):
        total = mine[...] + other[...].astype(F32)
        first = total[:, :hidw]
        first = put_parts(first, hid, [pick_whole(first, hid)])
        total = jnp.concatenate([first, total[:, hidw:]], axis=-1)
        return total, total

    mine, other = fused(add_squares, three_half, mine, core_swap(other))
    landed = chip_swap(other)
    arrived, landed = lax.optimization_barrier((arrived, landed))
    mine_l, other_l, cot_u, norm_scales = fused(
        forward_lower,
        two_half + [((block, wide), BF), ((block, 128), F32)],
        core_s,
        arrived,
        gain,
        w_gate,
        w_up,
    )

    def own_quarter(values, chip):
        return jnp.where(chip == 0, values[:quarter], values[quarter:])

    def sigmoid(value):
        return 1.0 / (1.0 + jnp.exp(-value))

    def activate(chip, mine, landed):
        total = mine[...] + landed[...].astype(F32)
        kinds = [total[:, at * hidw : (at + 1) * hidw] for at in range(3)]
        scale = lax.rsqrt(pick_whole(kinds[0], hid) / D + EPSILON)
        gate = jnp.where(lanes(kinds[0].shape) < hid, kinds[0] * scale, 0.0)
        up_value = kinds[1] * scale
        sig = sigmoid(gate)
        act = gate * sig
        g_gate = rounded(kinds[2] * up_value * sig * (1.0 + gate * (1.0 - sig)))
        g_up = rounded(kinds[2] * act)
        inner = jnp.sum(g_gate * gate + g_up * up_value, axis=-1, keepdims=True)
        pair = jnp.concatenate([put_parts(g_gate, hid, [inner, scale]), g_up], axis=-1)
        scaled = jnp.concatenate([g_gate, g_up], axis=-1) * scale
        return pair, act * up_value, own_quarter(scaled, chip)

    pair, hidden_u, quarter_u = fused(
        activate,
        [((half, 2 * hidw), BF), ((half, hidw), BF), ((quarter, 2 * hidw), BF)],
        chip_s,
        mine,
        landed,
    )

    def activate_lower(mine, landed, hidden_u):
        total = mine[...] + landed[...].astype(F32)
        gate, up_value = total[:, :hidw], total[:, hidw:]
        scale = lax.rsqrt(pick_whole(gate, hid) / D + EPSILON)
        gate = jnp.where(lanes(gate.shape) < hid, gate * scale, 0.0)
        up_value = up_value * scale
        sig = sigmoid(gate)
        act = gate * sig
        slope = up_value * sig * (1.0 + gate * (1.0 - sig))
        hidden = jnp.concatenate([hidden_u[...].astype(F32), act * up_value], axis=-1)
        scales = jnp.broadcast_to(scale, (half, 128))
        return jnp.concatenate([gate, up_value, act, slope], axis=-1), scales, hidden

    def all_quarters(values):
        return lax.all_gather(values, ("segment", "dp"), axis=0, tiled=False)

    def normed_sums(core, mine, other, w_gate, w_up):
        both = joined(mine[...].astype(F32), other[...].astype(F32), core)
        g_gate, g_up = both[:, :hidw], both[:, hidw:]
        sums = dot(g_gate.astype(BF), w_gate[...]) + dot(g_up.astype(BF), w_up[...])
        sums = put_parts(sums, part, [pick_whole(g_gate, hid)])
        at = lanes((block, 128))
        scales = jnp.where(at >= 0, pick_whole(g_gate, hid + 2), 0.0)
        return sums.reshape(tp_count, rows, wide), scales

    normed_outs = [((tp_count, rows, wide), BF), ((block, 128), F32)]
    def quarter_inputs(dp, quarter_u, sections, norm_scales, pre_gain):
        begin = dp * quarter
        mine = [sections[kind, pl.ds(begin, quarter), :].astype(F32) for kind in range(3)]
        scale = pick(norm_scales[pl.ds(begin, quarter), :], 0)
        inject = mine[0] * scale * pre_gain[...]
        kinds = [quarter_u[...].astype(F32), mine[2], mine[1], inject]
        return (jnp.concatenate(kinds, axis=-1),)

    (upper,) = fused(
        quarter_inputs,
        [((quarter, 2 * hidw + 3 * unit), BF)],
        dp_s,
        quarter_u,
        sections,
        norm_scales,
        pre_gain,
    )
    upper = all_quarters(upper)
    sent, scales = fused(normed_sums, normed_outs, core_s, pair, core_swap(pair), w_gate, w_up)
    arrived = exchange(sent, "tensor")

    def mixed_back(tp, arrived, cot, mixed, scales, gain):
        sums = jnp.sum(arrived[...].astype(F32), axis=0)
        scale = pick(scales[pl.ds(tp * rows, rows), :], 0)
        inner = pick_whole(sums[:, :unit], part) / scale / D
        factor = gain[...]
        weighted = sums * factor
        g_mixed = rounded(
            cot + scale * weighted - mixed * (scale * scale * scale) * inner
        )
        gain_part = jnp.sum(jnp.where(factor > 0.0, sums * mixed * scale, 0.0), axis=0, keepdims=True)
        return g_mixed, gain_part

    def upper_back(tp, arrived, kept_8, scales, gain):
        mixed, cot = kept_8[0:rows, :], kept_8[2 * rows : 3 * rows, :]
        g_mixed, gain_part = mixed_back(tp, arrived, cot, mixed, scales, gain)
        spread = jnp.broadcast_to(g_mixed[None], (tp_count, rows, wide))
        gain_part = jnp.broadcast_to(gain_part, (rows, wide))
        return spread, jnp.concatenate([g_mixed, gain_part], axis=0), blocks_of(g_mixed)

    mine_l, other_l = fused(add_squares, two_half, mine_l, core_swap(other_l))
    landed_l = chip_swap(other_l)
    lower, half_scales, hidden = fused(
        activate_lower,
        [((half, 4 * hidw), F32), ((half, 128), F32), ((half, 2 * hidw), BF)],
        mine_l,
        landed_l,
        hidden_u,
    )
    hidden_other = core_swap(hidden)
    spread_shape = ((tp_count, rows, wide), BF)
    eight_blocks = ((group, rows, unit), BF)
    sent, upper_8, g_mixed_8 = fused(
        upper_back,
        [spread_shape, ((2 * rows, wide), F32), eight_blocks],
        tp_s,
        arrived,
        kept_8,
        scales,
        gain,
    )
    shared = lax.all_gather(
        jnp.concatenate(ready_8 + from_segments(g_mixed_8), axis=0), "tensor", axis=0, tiled=False
    )
    sent, other_l = lax.optimization_barrier((sent, other_l))
    arrived_u = exchange(sent, "tensor")

    def state_back(tp, arrived, w_state):
        g_mixed = arrived[...].astype(F32).reshape(block, wide).astype(BF)
        g_state = dot_t(g_mixed, w_state[...]).reshape(tp_count, 1, rows, unit)
        at = lax.broadcasted_iota(jnp.int32, (tp_count, dp_count, rows, unit), 1)
        return (
            jnp.where(at == tp // group, g_state, 0.0).reshape(tp_count * dp_count, rows, unit),
        )

    (sent,) = fused(
        state_back, [((tp_count * dp_count, rows, unit), BF)], tp_s, arrived_u, w_state
    )
    sent, lower = lax.optimization_barrier((sent, lower))
    arrived = exchange(sent, ("tensor", "dp"))

    def lower_cot(dp, arrived):
        blocks = []
        for at in range(group):
            first = (dp * group + at) * dp_count
            blocks.append(sum(arrived[first + one].astype(F32) for one in range(dp_count)))
        cot = rounded(jnp.concatenate(blocks, axis=-1))
        return jnp.broadcast_to(cot[None], (tp_count, rows, wide)), cot

    sent, cot_l8 = fused(lower_cot, [spread_shape, eight], dp_s, arrived)
    sent, hidden_other = lax.optimization_barrier((sent, hidden_other))
    arrived_c = exchange(sent, "tensor")

    def hidden_back(core, arrived, w_down):
        cot = arrived[...].astype(F32).reshape(block, wide).astype(BF)
        return halves(dot_t(cot, w_down[...]), core)

    one_half = [((half, hidw), F32), ((half, hidw), BF)]
    mine, other = fused(hidden_back, one_half, core_s, arrived_c, w_down)

    def add(mine, other):
        total = mine[...] + other[...].astype(F32)
        return total, total

    mine, other = fused(add, one_half, mine, core_swap(other))
    landed = chip_swap(other)

    def lower_hidden(chip, mine, landed, lower, scales):
        g_hidden = mine[...] + landed[...].astype(F32)
        gate, up_value, act, slope = (lower[:, at * hidw : (at + 1) * hidw] for at in range(4))
        g_gate = rounded(g_hidden * slope)
        g_up = rounded(g_hidden * act)
        inner = jnp.sum(g_gate * gate + g_up * up_value, axis=-1, keepdims=True)
        scale = pick(scales[...], 0)
        pair = jnp.concatenate([put_parts(g_gate, hid, [inner, scale]), g_up], axis=-1)
        scaled = jnp.concatenate([g_gate, g_up], axis=-1) * scale
        return pair, own_quarter(scaled, chip)

    pair, quarter_l = fused(
        lower_hidden,
        [((half, 2 * hidw), BF), ((quarter, 2 * hidw), BF)],
        chip_s,
        mine,
        landed,
        lower,
        half_scales,
    )
    sent, scales = fused(normed_sums, normed_outs, core_s, pair, core_swap(pair), w_gate, w_up)

    def down_part(core, mine, other, cot_u, arrived_c):
        hidden = joined(mine[...].astype(F32), other[...].astype(F32), core)
        first, second = hidden[:, :hidw].T.astype(BF), hidden[:, hidw:].T.astype(BF)
        cot_l = arrived_c[...].astype(F32).reshape(block, wide).astype(BF)
        blocks = []
        for at in range(group):
            cut = slice(at * unit, (at + 1) * unit)
            blocks.append((dot(first, cot_u[:, cut]) + dot(second, cot_l[:, cut]))[None])
        return (jnp.concatenate(blocks, axis=0),)

    (down,) = fused(
        down_part, [((group, hidw, unit), BF)], core_s, hidden, hidden_other, cot_u, arrived_c
    )
    down = lax.psum_scatter(down, "segment", scatter_dimension=0, tiled=True)
    arrived = exchange(sent, "tensor")

    def two_rows(value, count):
        high = rounded(value)
        at = lax.broadcasted_iota(jnp.int32, (count, value.shape[1]), 0)
        return jnp.where(at == 0, high, jnp.where(at == 1, value - high, 0.0))

    def lower_back(tp, arrived, cot_8, kept_8, scales, gain, upper_8):
        mixed, prior = kept_8[rows : 2 * rows, :], kept_8[3 * rows :, :]
        g_mixed, gain_part = mixed_back(tp, arrived, cot_8[...], mixed, scales, gain)
        inner = jnp.sum((upper_8[0:rows, :] + g_mixed) * prior, axis=-1, keepdims=True)
        total = upper_8[rows : rows + 1, :] + gain_part
        own = jnp.concatenate([put_parts(g_mixed, part, [inner]), two_rows(total, rows)], axis=0)
        return jnp.broadcast_to(own[None], (tp_count, 2 * rows, wide)), blocks_of(g_mixed)

    sent, g_mixed_8 = fused(
        lower_back,
        [((tp_count, 2 * rows, wide), BF), eight_blocks],
        tp_s,
        arrived,
        cot_l8,
        kept_8,
        scales,
        gain,
        upper_8,
    )
    g_mixed_8 = jnp.concatenate(from_segments(g_mixed_8), axis=0)
    sent, upper = lax.optimization_barrier((sent, upper))
    arrived = exchange(sent, "tensor")
    arrived, g_mixed_8 = lax.optimization_barrier((arrived, g_mixed_8))
    lower_shared = exchange(jnp.broadcast_to(g_mixed_8[None], (tp_count,) + g_mixed_8.shape), "tensor")

    def inject_back(core, arrived, arrived_u, w_inject, gain, sections, norm_scales):
        every = arrived[...].astype(F32)
        lower_f = every[:, :rows].reshape(block, wide)
        inner = pick_whole(lower_f[:, :unit], part)
        g_mixed_l = jnp.where(gain[...] > 0.0, lower_f, 0.0).astype(BF)
        g_mixed_u = arrived_u[...].astype(F32).reshape(block, wide).astype(BF)
        sums = dot_t(g_mixed_u, w_inject[...]) + dot_t(g_mixed_l, w_inject[...])
        mine, other = halves(put_parts(sums, part, [inner]), core)
        prelude = sections[0].astype(F32)
        gain_row = jnp.sum(sums * prelude * pick(norm_scales[...], 0), axis=0, keepdims=True)
        mine = jnp.concatenate([mine, two_rows(gain_row, 16)], axis=0)
        other = jnp.concatenate([other, two_rows(gain_row, 16)], axis=0)
        gains = jnp.sum(every[:, rows:], axis=0)
        gains = gains[0:1] + gains[1:2]
        return mine, other, blocks_of(two_rows(gains, 16))

    more = half + 16
    one_part = [((more, unit), F32), ((more, unit), BF)]
    mine, other, last = fused(
        inject_back,
        one_part + [((group, 16, unit), BF)],
        core_s,
        arrived,
        arrived_u,
        w_inject,
        gain,
        sections,
        norm_scales,
    )

    def add_inner(mine, other):
        total = mine[...] + other[...].astype(F32)
        sums = put_parts(total[:half], part, [pick_whole(total[:half], part)])
        gain_row = total[half : half + 1] + total[half + 1 : half + 2]
        total = jnp.concatenate([sums, two_rows(gain_row, 16)], axis=0)
        return total, total

    mine, other = fused(add_inner, one_part, mine, core_swap(other))
    landed = chip_swap(other)

    def prelude_back(core, chip, mine, landed, sections, norm_scales, pre_gain, cot, last):
        total = mine[...] + landed[...].astype(F32)
        gain_row = total[half : half + 1] + total[half + 1 : half + 2]
        total = total[:half]
        inner = pick_whole(total, part) / D
        prelude, _ = halves(sections[0].astype(F32), core)
        scale, _ = halves(norm_scales[...], core)
        scale = pick(scale, 0)
        scaled = total * pre_gain[...]
        grad = scale * scaled - prelude * (scale * scale * scale) * inner
        top_scale = pick(norm_scales[...], 1)
        coda_row = jnp.sum(
            cot[...].astype(F32) * sections[3].astype(F32) * top_scale, axis=0, keepdims=True
        )
        own = jnp.concatenate(
            [own_quarter(grad, chip), two_rows(gain_row, 8), two_rows(coda_row, 8)], axis=0
        ).astype(BF)
        own = jnp.broadcast_to(own[None], (group,) + own.shape)
        return (jnp.concatenate([last[...], own], axis=1),)

    (last,) = fused(
        prelude_back,
        [((group, 32 + quarter, unit), BF)],
        core_s,
        chip_s,
        mine,
        landed,
        sections,
        norm_scales,
        pre_gain,
        cot,
        last,
    )
    last, lower_shared = lax.optimization_barrier((last, lower_shared))
    last = exchange(last, "segment")

    lower_all = all_quarters(quarter_l)

    def hidden_grads(seg, shared, upper, lower):
        total = 0.0
        every = shared[...].astype(F32)
        for step in range(seg_count):
            begin = lax.rem(seg + seg_count - step, seg_count) * dp_count
            for number, source in enumerate((upper, lower)):
                first = (2 * step + number) * rows
                left = every[:, first : first + rows].reshape(block, unit).T.astype(BF)
                right = source[pl.ds(begin, dp_count), :, : 2 * hidw].astype(F32)
                total = total + dot(left, right.reshape(block, 2 * hidw).astype(BF))
        return total[:part, :hid], total[:part, hidw : hidw + hid]

    seg_s = seg_index.reshape(1)
    grad_gate, grad_up = fused(
        hidden_grads, [((part, hid), BF), ((part, hid), BF)], seg_s, shared, upper, lower_all
    )

    def adapter_grads(seg, upper, shared, lower_shared):
        g_state, g_inject = 0.0, 0.0
        uppers = shared[...].astype(F32)[:, 2 * seg_count * rows :]
        lowers = lower_shared[...].astype(F32)
        for step in range(seg_count):
            begin = lax.rem(seg + seg_count - step, seg_count) * dp_count
            cut = slice(step * rows, (step + 1) * rows)
            right_u = uppers[:, cut].reshape(block, unit).astype(BF)
            right_l = lowers[:, cut].reshape(block, unit).astype(BF)
            kinds = [
                turned(
                    upper[pl.ds(begin, dp_count), :, first : first + unit]
                    .astype(F32)
                    .reshape(block, unit)
                )
                for first in range(2 * hidw, 2 * hidw + 3 * unit, unit)
            ]
            g_state = g_state + dot(kinds[0], right_u) + dot(kinds[1], right_l)
            g_inject = g_inject + dot(kinds[2], right_u) + dot(kinds[2], right_l)
        return g_state[:part, :part], g_inject[:part, :part]

    grad_state, grad_inject = fused(
        adapter_grads,
        [((part, part), BF), ((part, part), BF)],
        seg_s,
        upper,
        shared,
        lower_shared,
    )

    def finish(last):
        tail = sum(last[at].astype(F32) for at in range(seg_count))
        begin = 16 + quarter
        gains = [tail[row : row + 1] + tail[row + 1 : row + 2] for row in (0, begin, begin + 8)]
        prelude = [last[at].astype(F32)[16 : 16 + quarter] for at in range(seg_count)]
        prelude = turned(jnp.concatenate(prelude, axis=0))[:part]
        return *gains, prelude

    row = ((1, unit), F32)
    mlp_row, prelude_row, coda_row, out_prelude = fused(
        finish, [row, row, row, ((part, block), BF)], last
    )
    return (
        out_prelude.T,
        prelude_row[0, :part],
        coda_row[0, :part],
        grad_state,
        grad_inject,
        grad_gate,
        grad_up,
        down[0, :hid, :part],
        mlp_row[0, :part].astype(BF),
    )


def solution(mesh):
    placed = (
        P("segment", "dp", "tensor"),
        P("dp", "tensor"),
        P("tensor"),
        P("tensor"),
        P("dp"),
        P("tensor", "dp"),
        P("tensor", "dp"),
        P("dp", "tensor"),
        P("dp", "tensor"),
        P("tensor", "dp"),
    )
    return jax.shard_map(
        local,
        mesh=mesh,
        in_specs=placed,
        out_specs=(
            P("dp", "tensor"),
            P("tensor"),
            P("tensor"),
            P("tensor", ("dp", "segment")),
            P("tensor", ("dp", "segment")),
            P(("dp", "segment"), "tensor"),
            P(("dp", "segment"), "tensor"),
            P("tensor", ("dp", "segment")),
            P(("dp", "segment")),
        ),
        check_vma=False,
    )
```

```python
import jax
import jax.numpy as jnp
from jax import lax
from jax.experimental import pallas as pl
from jax.experimental.pallas import tpu as pltpu
from jax.sharding import PartitionSpec as P

D = 5280
EPSILON = 1e-06
BF = jnp.bfloat16
F32 = jnp.float32
LIMIT = 24 * 1024 * 1024


def up(value):
    return -(-value // 128) * 128


def dot(left, right):
    return jnp.dot(left, right, preferred_element_type=F32)


def dot_t(left, right):
    return lax.dot_general(left, right, (((1,), (1,)), ((), ())), preferred_element_type=F32)


def turned(value):
    return value.astype(F32).T.astype(BF)


def rounded(value):
    return value.astype(BF).astype(F32)


def lanes(shape):
    return lax.broadcasted_iota(jnp.int32, shape, len(shape) - 1)


def pick(value, lane):
    return jnp.sum(jnp.where(lanes(value.shape) == lane, value, 0.0), axis=-1, keepdims=True)


def pick_whole(value, lane):
    at = lanes(value.shape)
    return jnp.sum(jnp.where((at == lane) | (at == lane + 1), value, 0.0), axis=-1, keepdims=True)


def put_parts(value, lane, scalars):
    at = lanes(value.shape)
    for number, scalar in enumerate(scalars):
        high = rounded(scalar)
        value = jnp.where(at == lane + 2 * number, high, value)
        value = jnp.where(at == lane + 2 * number + 1, scalar - high, value)
    return value


def fused(body, outs, *args):
    scalar = [arg.dtype == jnp.int32 for arg in args]

    def kernel(*refs):
        given = [ref[0] if is_scalar else ref for ref, is_scalar in zip(refs, scalar)]
        results = body(*given)
        for ref, value in zip(refs[len(args) :], results):
            if value is not None:
                if value.shape == ref.shape:
                    ref[...] = value.astype(ref.dtype)
                else:
                    ref[...] = jnp.zeros(ref.shape, ref.dtype)
                    ref[tuple(slice(0, size) for size in value.shape)] = value.astype(ref.dtype)

    specs = [
        pl.BlockSpec(memory_space=pltpu.SMEM if is_scalar else pltpu.VMEM) for is_scalar in scalar
    ]
    return pl.pallas_call(
        kernel,
        out_shape=[jax.ShapeDtypeStruct(shape, kind) for shape, kind in outs],
        in_specs=specs,
        out_specs=[pl.BlockSpec(memory_space=pltpu.VMEM) for _ in outs],
        compiler_params=pltpu.CompilerParams(vmem_limit_bytes=LIMIT),
    )(*args)


def exchange(values, axis):
    return lax.all_to_all(values, axis, 0, 0, tiled=True)


def core_swap(values):
    return lax.ppermute(values, "dp", [(0, 1), (1, 0), (2, 3), (3, 2)])


def chip_swap(values):
    return lax.ppermute(values, "dp", [(0, 2), (2, 0), (1, 3), (3, 1)])


def rotate(values, step):
    return lax.ppermute(values, "segment", [(at, (at + step) % 4) for at in range(4)])


def halves(values, core):
    count, width = values.shape
    blocks = values.reshape(2, 2, count // 4, width)
    first, second = blocks[:, 0].reshape(count // 2, width), blocks[:, 1].reshape(count // 2, width)
    return jnp.where(core == 0, first, second), jnp.where(core == 0, second, first)


def joined(mine, other, core):
    count, width = mine.shape
    first = jnp.where(core == 0, mine, other).reshape(2, 1, count // 2, width)
    second = jnp.where(core == 0, other, mine).reshape(2, 1, count // 2, width)
    return jnp.concatenate([first, second], axis=1).reshape(2 * count, width)


def gathered_blocks(values, core, chip):
    other = core_swap(values)
    two = jnp.stack([jnp.where(core == 0, values, other), jnp.where(core == 0, other, values)])
    far = chip_swap(two)
    four = jnp.stack([jnp.where(chip == 0, two, far), jnp.where(chip == 0, far, two)])
    return four.reshape((4 * values.shape[0],) + values.shape[1:])


def local(
    checkpoints,
    cot_out,
    prelude_gain,
    coda_gain,
    mlp_gain,
    adapt_state,
    adapt_inject,
    mlp_gate,
    mlp_up,
    mlp_down,
):
    dp_count = lax.axis_size("dp")
    seg_count = lax.axis_size("segment")
    tp_count = lax.axis_size("tensor")
    dp_index = lax.axis_index("dp").astype(jnp.int32)
    seg_index = lax.axis_index("segment").astype(jnp.int32)
    tp_index = lax.axis_index("tensor").astype(jnp.int32)
    core = dp_index % 2
    chip = dp_index // 2
    block = checkpoints.shape[1]
    quarter = block // seg_count
    half = 2 * quarter
    part = checkpoints.shape[2]
    unit = up(part + 8)
    hid = mlp_gate.shape[1]
    hidw = up(hid + 8)
    group = mlp_gain.shape[0] // part
    wide = group * unit
    rows = block // tp_count
    core_s, chip_s, dp_s, tp_s = (x.reshape(1) for x in (core, chip, dp_index, tp_index))

    def padded(values, axis, width):
        return jnp.pad(
            values,
            [(0, width - size) if at == axis else (0, 0) for at, size in enumerate(values.shape)],
        )

    def grouped(values, axis):
        shape = values.shape[:axis] + (group, part) + values.shape[axis + 1 :]
        values = padded(values.reshape(shape), axis + 1, unit)
        return values.reshape(shape[:axis] + (wide,) + shape[axis + 2 :])

    chunks = padded(checkpoints[0], 1, unit).reshape(seg_count, 1, quarter, unit)
    chunks = jnp.broadcast_to(chunks, (seg_count, dp_count, quarter, unit))
    sections = exchange(
        chunks.reshape(seg_count * dp_count, quarter, unit), ("segment", "dp")
    ).reshape(4, block, unit)
    cot_own = lax.dynamic_slice_in_dim(cot_out, seg_index * quarter, quarter, 0)
    cot = gathered_blocks(padded(cot_own, 1, unit), core, chip)
    pre_gain = padded(prelude_gain[None], 1, unit)
    cod_gain = padded(coda_gain[None], 1, unit)
    gain = grouped(mlp_gain[None], 1)

    def by_columns(weight):
        count, width = weight.shape
        blocks = []
        for at in range(group):
            row = lax.broadcasted_iota(jnp.int32, (width, unit), 0)
            col = lax.broadcasted_iota(jnp.int32, (width, unit), 1)
            chosen = jnp.where((row == col + at * part) & (col < part), 1.0, 0.0).astype(BF)
            blocks.append(dot(weight[...], chosen))
        return (jnp.concatenate(blocks, axis=-1),)

    def columns(weight, count):
        return fused(by_columns, [((count, wide), BF)], weight)[0]

    w_state = columns(adapt_state, unit)
    w_inject = columns(adapt_inject, unit)
    w_gate = columns(mlp_gate.T, hidw)
    w_up = columns(mlp_up.T, hidw)
    w_down = columns(mlp_down, hidw)

    def adapter(sections, cot, pre_gain, cod_gain, w_state, w_inject):
        prelude, lower, upper, top = (sections[at].astype(F32) for at in range(4))
        cot_f = cot[...].astype(F32)
        cut = (tp_count, rows, unit)
        left = jnp.concatenate([upper.reshape(cut), lower.reshape(cut)], axis=1)
        left = left.reshape(2 * block, unit).astype(BF)
        states = dot(left, w_state[...]).reshape(tp_count, 2 * rows, wide)
        prior = dot((prelude * pre_gain[...]).astype(BF), w_inject[...]).reshape(tp_count, rows, wide)
        row_sums = [
            jnp.sum(prelude * prelude, axis=-1, keepdims=True),
            jnp.sum(top * top, axis=-1, keepdims=True),
            jnp.sum(cot_f * cod_gain[...] * top, axis=-1, keepdims=True),
        ]
        sums = put_parts(jnp.zeros((block, unit), F32), 0, row_sums)
        coda = cod_gain[...]
        high = rounded(coda)
        at = lax.broadcasted_iota(jnp.int32, (rows, unit), 0)
        gains = jnp.where(at == 0, high, jnp.where(at == 1, coda - high, 0.0))
        gains = jnp.broadcast_to(gains[None], cut)
        extra = jnp.concatenate(
            [top.reshape(cut), cot_f.reshape(cut), gains, sums.reshape(cut)], axis=-1
        )
        return (jnp.concatenate([states, prior, extra], axis=1),)

    (sent,) = fused(
        adapter,
        [((tp_count, 4 * rows, wide), BF)],
        sections,
        cot,
        pre_gain,
        cod_gain,
        w_state,
        w_inject,
    )
    arrived = exchange(sent, "tensor")

    arrived, w_gate, w_up, w_down = lax.optimization_barrier((arrived, w_gate, w_up, w_down))

    def blocks_of(value):
        return jnp.concatenate(
            [value[None, :, at * unit : (at + 1) * unit] for at in range(group)], axis=0
        )

    def mix(dp, arrived, gain):
        sums = jnp.sum(arrived[...].astype(F32), axis=0)
        totals = sums[3 * rows :, 3 * unit :]
        near = [arrived[dp * group + at].astype(F32)[3 * rows :] for at in range(group)]
        top = jnp.concatenate([value[:, :unit] for value in near], axis=-1)
        cot_f = jnp.concatenate([value[:, unit : 2 * unit] for value in near], axis=-1)
        coda = jnp.concatenate(
            [value[0:1, 2 * unit : 3 * unit] + value[1:2, 2 * unit : 3 * unit] for value in near], axis=-1
        )
        pre_scale = lax.rsqrt(pick_whole(totals, 0) / D + EPSILON)
        top_scale = lax.rsqrt(pick_whole(totals, 2) / D + EPSILON)
        inner = pick_whole(totals, 4) / D
        prior = sums[2 * rows : 3 * rows]
        mixed_u = rounded(sums[:rows] + pre_scale * prior)
        mixed_l = rounded(sums[rows : 2 * rows] + pre_scale * prior)
        cot_u = rounded(
            top_scale * (cot_f * coda) - top * (top_scale * top_scale * top_scale) * inner
        )
        own = jnp.concatenate(
            [put_parts(mixed_u, part, [pre_scale, top_scale]), mixed_l, cot_u], axis=0
        )
        spread = jnp.broadcast_to(own[None], (tp_count,) + own.shape)
        ready = jnp.concatenate([mixed_u, mixed_l], axis=0) * gain[...]
        kept = jnp.concatenate([mixed_u, mixed_l, cot_u, prior], axis=0)
        return spread, kept, blocks_of(ready)

    eight = ((rows, wide), F32)
    sent, kept_8, ready_8 = fused(
        mix,
        [((tp_count, 3 * rows, wide), BF), ((4 * rows, wide), F32), ((group, 2 * rows, unit), BF)],
        dp_s,
        arrived,
        gain,
    )

    def from_segments(values):
        return [lax.dynamic_index_in_dim(values, seg_index, 0, keepdims=False)] + [
            rotate(
                lax.dynamic_index_in_dim(values, (seg_index + step) % seg_count, 0, keepdims=False), step
            )
            for step in range(1, seg_count)
        ]

    ready_8 = jnp.concatenate(from_segments(ready_8), axis=0)
    arrived = exchange(sent, "tensor")
    arrived, ready_8 = lax.optimization_barrier((arrived, ready_8))

    def forward_upper(core, arrived, gain, w_gate, w_up, w_down):
        mixed = arrived[:, :rows, :].astype(F32).reshape(block, wide)
        cot_u = arrived[...].astype(F32)[:, 2 * rows :].reshape(block, wide).astype(BF)
        factor = gain[...]
        squares = jnp.sum(jnp.where(factor > 0.0, mixed * mixed, 0.0), axis=-1, keepdims=True)
        ready = (mixed * factor).astype(BF)
        sums = jnp.concatenate(
            [
                put_parts(dot_t(ready, w_gate[...]), hid, [squares]),
                dot_t(ready, w_up[...]),
                dot_t(cot_u, w_down[...]),
            ],
            axis=-1,
        )
        return halves(sums, core)

    def forward_lower(core, arrived, gain, w_gate, w_up):
        every = arrived[...].astype(F32)
        mixed_u = every[:, :rows].reshape(block, wide)
        mixed = every[:, rows : 2 * rows].reshape(block, wide)
        cot_u = every[:, 2 * rows :].reshape(block, wide)
        factor = gain[...]
        squares = jnp.sum(jnp.where(factor > 0.0, mixed * mixed, 0.0), axis=-1, keepdims=True)
        ready = (mixed * factor).astype(BF)
        sums = jnp.concatenate(
            [put_parts(dot_t(ready, w_gate[...]), hid, [squares]), dot_t(ready, w_up[...])], axis=-1
        )
        mine, other = halves(sums, core)
        scales = mixed_u[:, :unit]
        at = lanes((block, 128))
        scales = jnp.where(at == 0, pick_whole(scales, part), pick_whole(scales, part + 2))
        return mine, other, cot_u, scales

    three_half = [((half, 3 * hidw), F32), ((half, 3 * hidw), BF)]
    two_half = [((half, 2 * hidw), F32), ((half, 2 * hidw), BF)]
    mine, other = fused(forward_upper, three_half, core_s, arrived, gain, w_gate, w_up, w_down)

    def add_squares(mine, other):
        total = mine[...] + other[...].astype(F32)
        first = total[:, :hidw]
        first = put_parts(first, hid, [pick_whole(first, hid)])
        total = jnp.concatenate([first, total[:, hidw:]], axis=-1)
        return total, total

    mine, other = fused(add_squares, three_half, mine, core_swap(other))
    landed = chip_swap(other)
    arrived, landed = lax.optimization_barrier((arrived, landed))
    mine_l, other_l, cot_u, norm_scales = fused(
        forward_lower,
        two_half + [((block, wide), BF), ((block, 128), F32)],
        core_s,
        arrived,
        gain,
        w_gate,
        w_up,
    )

    def own_quarter(values, chip):
        return jnp.where(chip == 0, values[:quarter], values[quarter:])

    def sigmoid(value):
        return 1.0 / (1.0 + jnp.exp(-value))

    def activate(chip, mine, landed):
        total = mine[...] + landed[...].astype(F32)
        kinds = [total[:, at * hidw : (at + 1) * hidw] for at in range(3)]
        scale = lax.rsqrt(pick_whole(kinds[0], hid) / D + EPSILON)
        gate = jnp.where(lanes(kinds[0].shape) < hid, kinds[0] * scale, 0.0)
        up_value = kinds[1] * scale
        sig = sigmoid(gate)
        act = gate * sig
        g_gate = rounded(kinds[2] * up_value * sig * (1.0 + gate * (1.0 - sig)))
        g_up = rounded(kinds[2] * act)
        inner = jnp.sum(g_gate * gate + g_up * up_value, axis=-1, keepdims=True)
        pair = jnp.concatenate([put_parts(g_gate, hid, [inner, scale]), g_up], axis=-1)
        scaled = jnp.concatenate([g_gate, g_up], axis=-1) * scale
        return pair, act * up_value, own_quarter(scaled, chip)

    pair, hidden_u, quarter_u = fused(
        activate,
        [((half, 2 * hidw), BF), ((half, hidw), BF), ((quarter, 2 * hidw), BF)],
        chip_s,
        mine,
        landed,
    )

    def activate_lower(mine, landed, hidden_u):
        total = mine[...] + landed[...].astype(F32)
        gate, up_value = total[:, :hidw], total[:, hidw:]
        scale = lax.rsqrt(pick_whole(gate, hid) / D + EPSILON)
        gate = jnp.where(lanes(gate.shape) < hid, gate * scale, 0.0)
        up_value = up_value * scale
        sig = sigmoid(gate)
        act = gate * sig
        slope = up_value * sig * (1.0 + gate * (1.0 - sig))
        hidden = jnp.concatenate([hidden_u[...].astype(F32), act * up_value], axis=-1)
        scales = jnp.broadcast_to(scale, (half, 128))
        return jnp.concatenate([gate, up_value, act, slope], axis=-1), scales, hidden

    def all_quarters(values):
        return lax.all_gather(values, ("segment", "dp"), axis=0, tiled=False)

    def normed_sums(core, mine, other, w_gate, w_up):
        both = joined(mine[...].astype(F32), other[...].astype(F32), core)
        g_gate, g_up = both[:, :hidw], both[:, hidw:]
        sums = dot(g_gate.astype(BF), w_gate[...]) + dot(g_up.astype(BF), w_up[...])
        sums = put_parts(sums, part, [pick_whole(g_gate, hid)])
        at = lanes((block, 128))
        scales = jnp.where(at >= 0, pick_whole(g_gate, hid + 2), 0.0)
        return sums.reshape(tp_count, rows, wide), scales

    normed_outs = [((tp_count, rows, wide), BF), ((block, 128), F32)]
    def quarter_inputs(dp, quarter_u, sections, norm_scales, pre_gain):
        begin = dp * quarter
        mine = [sections[kind, pl.ds(begin, quarter), :].astype(F32) for kind in range(3)]
        scale = pick(norm_scales[pl.ds(begin, quarter), :], 0)
        inject = mine[0] * scale * pre_gain[...]
        kinds = [quarter_u[...].astype(F32), mine[2], mine[1], inject]
        return (jnp.concatenate(kinds, axis=-1),)

    (upper,) = fused(
        quarter_inputs,
        [((quarter, 2 * hidw + 3 * unit), BF)],
        dp_s,
        quarter_u,
        sections,
        norm_scales,
        pre_gain,
    )
    sent, scales = fused(normed_sums, normed_outs, core_s, pair, core_swap(pair), w_gate, w_up)
    arrived = exchange(sent, "tensor")
    arrived, upper, ready_8 = lax.optimization_barrier((arrived, upper, ready_8))
    upper = all_quarters(upper)
    shared = lax.all_gather(
        jnp.pad(ready_8, ((0, 4 * rows), (0, 0))), "tensor", axis=0, tiled=False
    )

    def mixed_back(tp, arrived, cot, mixed, scales, gain):
        sums = jnp.sum(arrived[...].astype(F32), axis=0)
        scale = pick(scales[pl.ds(tp * rows, rows), :], 0)
        inner = pick_whole(sums[:, :unit], part) / scale / D
        factor = gain[...]
        weighted = sums * factor
        g_mixed = rounded(
            cot + scale * weighted - mixed * (scale * scale * scale) * inner
        )
        gain_part = jnp.sum(jnp.where(factor > 0.0, sums * mixed * scale, 0.0), axis=0, keepdims=True)
        return g_mixed, gain_part

    def upper_back(tp, arrived, kept_8, scales, gain):
        mixed, cot = kept_8[0:rows, :], kept_8[2 * rows : 3 * rows, :]
        g_mixed, gain_part = mixed_back(tp, arrived, cot, mixed, scales, gain)
        spread = jnp.broadcast_to(g_mixed[None], (tp_count, rows, wide))
        gain_part = jnp.broadcast_to(gain_part, (rows, wide))
        return spread, jnp.concatenate([g_mixed, gain_part], axis=0)

    mine_l, other_l = fused(add_squares, two_half, mine_l, core_swap(other_l))
    landed_l = chip_swap(other_l)
    lower, half_scales, hidden = fused(
        activate_lower,
        [((half, 4 * hidw), F32), ((half, 128), F32), ((half, 2 * hidw), BF)],
        mine_l,
        landed_l,
        hidden_u,
    )
    hidden_other = core_swap(hidden)
    spread_shape = ((tp_count, rows, wide), BF)
    sent, upper_8 = fused(
        upper_back,
        [spread_shape, ((2 * rows, wide), F32)],
        tp_s,
        arrived,
        kept_8,
        scales,
        gain,
    )
    sent, other_l = lax.optimization_barrier((sent, other_l))
    arrived_u = exchange(sent, "tensor")

    def state_back(tp, arrived, w_state):
        g_mixed = arrived[...].astype(F32).reshape(block, wide).astype(BF)
        g_state = dot_t(g_mixed, w_state[...]).reshape(tp_count, 1, rows, unit)
        at = lax.broadcasted_iota(jnp.int32, (tp_count, dp_count, rows, unit), 1)
        return (
            jnp.where(at == tp // group, g_state, 0.0).reshape(tp_count * dp_count, rows, unit),
        )

    (sent,) = fused(
        state_back, [((tp_count * dp_count, rows, unit), BF)], tp_s, arrived_u, w_state
    )
    sent, lower = lax.optimization_barrier((sent, lower))
    arrived = exchange(sent, ("tensor", "dp"))

    def lower_cot(dp, arrived):
        blocks = []
        for at in range(group):
            first = (dp * group + at) * dp_count
            blocks.append(sum(arrived[first + one].astype(F32) for one in range(dp_count)))
        cot = rounded(jnp.concatenate(blocks, axis=-1))
        return jnp.broadcast_to(cot[None], (tp_count, rows, wide)), cot

    sent, cot_l8 = fused(lower_cot, [spread_shape, eight], dp_s, arrived)
    sent, hidden_other = lax.optimization_barrier((sent, hidden_other))
    arrived_c = exchange(sent, "tensor")

    def hidden_back(core, arrived, w_down):
        cot = arrived[...].astype(F32).reshape(block, wide).astype(BF)
        return halves(dot_t(cot, w_down[...]), core)

    one_half = [((half, hidw), F32), ((half, hidw), BF)]
    mine, other = fused(hidden_back, one_half, core_s, arrived_c, w_down)

    def add(mine, other):
        total = mine[...] + other[...].astype(F32)
        return total, total

    mine, other = fused(add, one_half, mine, core_swap(other))
    landed = chip_swap(other)

    def lower_hidden(chip, mine, landed, lower, scales):
        g_hidden = mine[...] + landed[...].astype(F32)
        gate, up_value, act, slope = (lower[:, at * hidw : (at + 1) * hidw] for at in range(4))
        g_gate = rounded(g_hidden * slope)
        g_up = rounded(g_hidden * act)
        inner = jnp.sum(g_gate * gate + g_up * up_value, axis=-1, keepdims=True)
        scale = pick(scales[...], 0)
        pair = jnp.concatenate([put_parts(g_gate, hid, [inner, scale]), g_up], axis=-1)
        scaled = jnp.concatenate([g_gate, g_up], axis=-1) * scale
        return pair, own_quarter(scaled, chip)

    pair, quarter_l = fused(
        lower_hidden,
        [((half, 2 * hidw), BF), ((quarter, 2 * hidw), BF)],
        chip_s,
        mine,
        landed,
        lower,
        half_scales,
    )
    sent, scales = fused(normed_sums, normed_outs, core_s, pair, core_swap(pair), w_gate, w_up)

    def down_part(core, mine, other, cot_u, arrived_c):
        hidden = joined(mine[...].astype(F32), other[...].astype(F32), core)
        first, second = hidden[:, :hidw].T.astype(BF), hidden[:, hidw:].T.astype(BF)
        cot_l = arrived_c[...].astype(F32).reshape(block, wide).astype(BF)
        blocks = []
        for at in range(group):
            cut = slice(at * unit, (at + 1) * unit)
            total = dot(first, cot_u[:, cut]) + dot(second, cot_l[:, cut])
            blocks.append(total[:hid, :part][None])
        return (jnp.concatenate(blocks, axis=0),)

    sent, hidden, hidden_other = lax.optimization_barrier((sent, hidden, hidden_other))
    (down,) = fused(
        down_part, [((group, hid, part), BF)], core_s, hidden, hidden_other, cot_u, arrived_c
    )
    down = lax.psum_scatter(down, "segment", scatter_dimension=0, tiled=True)
    arrived = exchange(sent, "tensor")

    def two_rows(value, count):
        high = rounded(value)
        at = lax.broadcasted_iota(jnp.int32, (count, value.shape[1]), 0)
        return jnp.where(at == 0, high, jnp.where(at == 1, value - high, 0.0))

    def lower_back(tp, arrived, cot_8, kept_8, scales, gain, upper_8):
        mixed, prior = kept_8[rows : 2 * rows, :], kept_8[3 * rows :, :]
        g_mixed, gain_part = mixed_back(tp, arrived, cot_8[...], mixed, scales, gain)
        inner = jnp.sum((upper_8[0:rows, :] + g_mixed) * prior, axis=-1, keepdims=True)
        total = upper_8[rows : rows + 1, :] + gain_part
        own = jnp.concatenate([put_parts(g_mixed, part, [inner]), two_rows(total, rows)], axis=0)
        both = jnp.concatenate([upper_8[0:rows, :], g_mixed], axis=0)
        return jnp.broadcast_to(own[None], (tp_count, 2 * rows, wide)), blocks_of(both)

    sent, g_mixed_8 = fused(
        lower_back,
        [((tp_count, 2 * rows, wide), BF), ((group, 2 * rows, unit), BF)],
        tp_s,
        arrived,
        cot_l8,
        kept_8,
        scales,
        gain,
        upper_8,
    )
    g_mixed_8 = jnp.concatenate(from_segments(g_mixed_8), axis=0)
    sent, upper = lax.optimization_barrier((sent, upper))
    arrived = exchange(sent, "tensor")
    arrived, g_mixed_8 = lax.optimization_barrier((arrived, g_mixed_8))
    lower_shared = exchange(jnp.broadcast_to(g_mixed_8[None], (tp_count,) + g_mixed_8.shape), "tensor")

    def inject_back(core, arrived, arrived_u, w_inject, gain, sections, norm_scales):
        every = arrived[...].astype(F32)
        lower_f = every[:, :rows].reshape(block, wide)
        inner = pick_whole(lower_f[:, :unit], part)
        g_mixed_l = jnp.where(gain[...] > 0.0, lower_f, 0.0).astype(BF)
        g_mixed_u = arrived_u[...].astype(F32).reshape(block, wide).astype(BF)
        sums = dot_t(g_mixed_u, w_inject[...]) + dot_t(g_mixed_l, w_inject[...])
        mine, other = halves(put_parts(sums, part, [inner]), core)
        prelude = sections[0].astype(F32)
        gain_row = jnp.sum(sums * prelude * pick(norm_scales[...], 0), axis=0, keepdims=True)
        mine = jnp.concatenate([mine, two_rows(gain_row, 16)], axis=0)
        other = jnp.concatenate([other, two_rows(gain_row, 16)], axis=0)
        gains = jnp.sum(every[:, rows:], axis=0)
        gains = gains[0:1] + gains[1:2]
        return mine, other, blocks_of(two_rows(gains, 16))

    more = half + 16
    one_part = [((more, unit), F32), ((more, unit), BF)]
    mine, other, last = fused(
        inject_back,
        one_part + [((group, 16, unit), BF)],
        core_s,
        arrived,
        arrived_u,
        w_inject,
        gain,
        sections,
        norm_scales,
    )

    def add_inner(mine, other):
        total = mine[...] + other[...].astype(F32)
        sums = put_parts(total[:half], part, [pick_whole(total[:half], part)])
        gain_row = total[half : half + 1] + total[half + 1 : half + 2]
        total = jnp.concatenate([sums, two_rows(gain_row, 16)], axis=0)
        return total, total

    mine, other = fused(add_inner, one_part, mine, core_swap(other))
    landed = chip_swap(other)

    def prelude_back(core, chip, mine, landed, sections, norm_scales, pre_gain, cot, last):
        total = mine[...] + landed[...].astype(F32)
        gain_row = total[half : half + 1] + total[half + 1 : half + 2]
        total = total[:half]
        inner = pick_whole(total, part) / D
        prelude, _ = halves(sections[0].astype(F32), core)
        scale, _ = halves(norm_scales[...], core)
        scale = pick(scale, 0)
        scaled = total * pre_gain[...]
        grad = scale * scaled - prelude * (scale * scale * scale) * inner
        top_scale = pick(norm_scales[...], 1)
        coda_row = jnp.sum(
            cot[...].astype(F32) * sections[3].astype(F32) * top_scale, axis=0, keepdims=True
        )
        own = jnp.concatenate(
            [own_quarter(grad, chip), two_rows(gain_row, 8), two_rows(coda_row, 8)], axis=0
        ).astype(BF)
        own = jnp.broadcast_to(own[None], (group,) + own.shape)
        return (jnp.concatenate([last[...], own], axis=1),)

    (last,) = fused(
        prelude_back,
        [((group, 32 + quarter, unit), BF)],
        core_s,
        chip_s,
        mine,
        landed,
        sections,
        norm_scales,
        pre_gain,
        cot,
        last,
    )
    last, lower_shared = lax.optimization_barrier((last, lower_shared))
    last = exchange(last, "segment")

    lower_all = all_quarters(quarter_l)

    def hidden_grads(seg, shared, upper, lower):
        total = 0.0
        every = shared[...].astype(F32)
        for step in range(seg_count):
            begin = lax.rem(seg + seg_count - step, seg_count) * dp_count
            for number, source in enumerate((upper, lower)):
                first = (2 * step + number) * rows
                left = every[:, first : first + rows].reshape(block, unit).T.astype(BF)
                right = source[pl.ds(begin, dp_count), :, : 2 * hidw].astype(F32)
                total = total + dot(left, right.reshape(block, 2 * hidw).astype(BF))
        return total[:part, :hid], total[:part, hidw : hidw + hid]

    seg_s = seg_index.reshape(1)
    grad_gate, grad_up = fused(
        hidden_grads, [((part, hid), BF), ((part, hid), BF)], seg_s, shared, upper, lower_all
    )

    def adapter_grads(seg, upper, lower_shared):
        g_state, g_inject = 0.0, 0.0
        every = lower_shared[...].astype(F32)
        for step in range(seg_count):
            begin = lax.rem(seg + seg_count - step, seg_count) * dp_count
            first = 2 * step * rows
            right_u = every[:, first : first + rows].reshape(block, unit).astype(BF)
            right_l = every[:, first + rows : first + 2 * rows].reshape(block, unit).astype(BF)
            kinds = [
                turned(
                    upper[pl.ds(begin, dp_count), :, first : first + unit]
                    .astype(F32)
                    .reshape(block, unit)
                )
                for first in range(2 * hidw, 2 * hidw + 3 * unit, unit)
            ]
            g_state = g_state + dot(kinds[0], right_u) + dot(kinds[1], right_l)
            g_inject = g_inject + dot(kinds[2], right_u) + dot(kinds[2], right_l)
        return g_state[:part, :part], g_inject[:part, :part]

    grad_state, grad_inject = fused(
        adapter_grads,
        [((part, part), BF), ((part, part), BF)],
        seg_s,
        upper,
        lower_shared,
    )

    def finish(last):
        tail = sum(last[at].astype(F32) for at in range(seg_count))
        begin = 16 + quarter
        gains = [tail[row : row + 1] + tail[row + 1 : row + 2] for row in (0, begin, begin + 8)]
        prelude = [last[at].astype(F32)[16 : 16 + quarter] for at in range(seg_count)]
        prelude = turned(jnp.concatenate(prelude, axis=0))[:part]
        return *gains, prelude

    row = ((1, unit), F32)
    mlp_row, prelude_row, coda_row, out_prelude = fused(
        finish, [row, row, row, ((part, block), BF)], last
    )
    return (
        out_prelude.T,
        prelude_row[0, :part],
        coda_row[0, :part],
        grad_state,
        grad_inject,
        grad_gate,
        grad_up,
        down[0],
        mlp_row[0, :part].astype(BF),
    )


def solution(mesh):
    placed = (
        P("segment", "dp", "tensor"),
        P("dp", "tensor"),
        P("tensor"),
        P("tensor"),
        P("dp"),
        P("tensor", "dp"),
        P("tensor", "dp"),
        P("dp", "tensor"),
        P("dp", "tensor"),
        P("tensor", "dp"),
    )
    return jax.shard_map(
        local,
        mesh=mesh,
        in_specs=placed,
        out_specs=(
            P("dp", "tensor"),
            P("tensor"),
            P("tensor"),
            P("tensor", ("dp", "segment")),
            P("tensor", ("dp", "segment")),
            P(("dp", "segment"), "tensor"),
            P(("dp", "segment"), "tensor"),
            P("tensor", ("dp", "segment")),
            P(("dp", "segment")),
        ),
        check_vma=False,
    )
```

```python
import jax
import jax.numpy as jnp
from jax import lax
from jax.experimental import pallas as pl
from jax.experimental.pallas import tpu as pltpu
from jax.sharding import PartitionSpec as P

D = 5280
EPSILON = 1e-06
BF = jnp.bfloat16
F32 = jnp.float32
LIMIT = 24 * 1024 * 1024


def up(value):
    return -(-value // 128) * 128


def dot(left, right):
    return jnp.dot(left, right, preferred_element_type=F32)


def dot_t(left, right):
    return lax.dot_general(left, right, (((1,), (1,)), ((), ())), preferred_element_type=F32)


def turned(value):
    return value.astype(F32).T.astype(BF)


def rounded(value):
    return value.astype(BF).astype(F32)


def lanes(shape):
    return lax.broadcasted_iota(jnp.int32, shape, len(shape) - 1)


def pick(value, lane):
    return jnp.sum(jnp.where(lanes(value.shape) == lane, value, 0.0), axis=-1, keepdims=True)


def pick_whole(value, lane):
    at = lanes(value.shape)
    return jnp.sum(jnp.where((at == lane) | (at == lane + 1), value, 0.0), axis=-1, keepdims=True)


def put_parts(value, lane, scalars):
    at = lanes(value.shape)
    for number, scalar in enumerate(scalars):
        high = rounded(scalar)
        value = jnp.where(at == lane + 2 * number, high, value)
        value = jnp.where(at == lane + 2 * number + 1, scalar - high, value)
    return value


def fused(body, outs, *args):
    scalar = [arg.dtype == jnp.int32 for arg in args]

    def kernel(*refs):
        given = [ref[0] if is_scalar else ref for ref, is_scalar in zip(refs, scalar)]
        results = body(*given)
        for ref, value in zip(refs[len(args) :], results):
            if value is not None:
                if value.shape == ref.shape:
                    ref[...] = value.astype(ref.dtype)
                else:
                    ref[...] = jnp.zeros(ref.shape, ref.dtype)
                    ref[tuple(slice(0, size) for size in value.shape)] = value.astype(ref.dtype)

    specs = [
        pl.BlockSpec(memory_space=pltpu.SMEM if is_scalar else pltpu.VMEM) for is_scalar in scalar
    ]
    return pl.pallas_call(
        kernel,
        out_shape=[jax.ShapeDtypeStruct(shape, kind) for shape, kind in outs],
        in_specs=specs,
        out_specs=[pl.BlockSpec(memory_space=pltpu.VMEM) for _ in outs],
        compiler_params=pltpu.CompilerParams(vmem_limit_bytes=LIMIT),
    )(*args)


def exchange(values, axis):
    return lax.all_to_all(values, axis, 0, 0, tiled=True)


def core_swap(values):
    return lax.ppermute(values, "dp", [(0, 1), (1, 0), (2, 3), (3, 2)])


def chip_swap(values):
    return lax.ppermute(values, "dp", [(0, 2), (2, 0), (1, 3), (3, 1)])


def rotate(values, step):
    return lax.ppermute(values, "segment", [(at, (at + step) % 4) for at in range(4)])


def halves(values, core):
    count, width = values.shape
    blocks = values.reshape(2, 2, count // 4, width)
    first, second = blocks[:, 0].reshape(count // 2, width), blocks[:, 1].reshape(count // 2, width)
    return jnp.where(core == 0, first, second), jnp.where(core == 0, second, first)


def joined(mine, other, core):
    count, width = mine.shape
    first = jnp.where(core == 0, mine, other).reshape(2, 1, count // 2, width)
    second = jnp.where(core == 0, other, mine).reshape(2, 1, count // 2, width)
    return jnp.concatenate([first, second], axis=1).reshape(2 * count, width)


def gathered_blocks(values, core, chip):
    other = core_swap(values)
    two = jnp.stack([jnp.where(core == 0, values, other), jnp.where(core == 0, other, values)])
    far = chip_swap(two)
    four = jnp.stack([jnp.where(chip == 0, two, far), jnp.where(chip == 0, far, two)])
    return four.reshape((4 * values.shape[0],) + values.shape[1:])


def local(
    checkpoints,
    cot_out,
    prelude_gain,
    coda_gain,
    mlp_gain,
    adapt_state,
    adapt_inject,
    mlp_gate,
    mlp_up,
    mlp_down,
):
    dp_count = lax.axis_size("dp")
    seg_count = lax.axis_size("segment")
    tp_count = lax.axis_size("tensor")
    dp_index = lax.axis_index("dp").astype(jnp.int32)
    seg_index = lax.axis_index("segment").astype(jnp.int32)
    tp_index = lax.axis_index("tensor").astype(jnp.int32)
    core = dp_index % 2
    chip = dp_index // 2
    block = checkpoints.shape[1]
    quarter = block // seg_count
    half = 2 * quarter
    part = checkpoints.shape[2]
    unit = up(part + 8)
    hid = mlp_gate.shape[1]
    hidw = up(hid + 8)
    group = mlp_gain.shape[0] // part
    wide = group * unit
    rows = block // tp_count
    core_s, chip_s, dp_s, tp_s = (x.reshape(1) for x in (core, chip, dp_index, tp_index))

    def padded(values, axis, width):
        return jnp.pad(
            values,
            [(0, width - size) if at == axis else (0, 0) for at, size in enumerate(values.shape)],
        )

    def grouped(values, axis):
        shape = values.shape[:axis] + (group, part) + values.shape[axis + 1 :]
        values = padded(values.reshape(shape), axis + 1, unit)
        return values.reshape(shape[:axis] + (wide,) + shape[axis + 2 :])

    chunks = padded(checkpoints[0], 1, unit).reshape(seg_count, 1, quarter, unit)
    chunks = jnp.broadcast_to(chunks, (seg_count, dp_count, quarter, unit))
    sections = exchange(
        chunks.reshape(seg_count * dp_count, quarter, unit), ("segment", "dp")
    ).reshape(4, block, unit)
    cot_own = lax.dynamic_slice_in_dim(cot_out, seg_index * quarter, quarter, 0)
    cot = gathered_blocks(padded(cot_own, 1, unit), core, chip)
    pre_gain = padded(prelude_gain[None], 1, unit)
    cod_gain = padded(coda_gain[None], 1, unit)
    gain = grouped(mlp_gain[None], 1)

    def by_columns(weight):
        count, width = weight.shape
        blocks = []
        for at in range(group):
            row = lax.broadcasted_iota(jnp.int32, (width, unit), 0)
            col = lax.broadcasted_iota(jnp.int32, (width, unit), 1)
            chosen = jnp.where((row == col + at * part) & (col < part), 1.0, 0.0).astype(BF)
            blocks.append(dot(weight[...], chosen))
        return (jnp.concatenate(blocks, axis=-1),)

    def columns(weight, count):
        return fused(by_columns, [((count, wide), BF)], weight)[0]

    w_state = columns(adapt_state, unit)
    w_inject = columns(adapt_inject, unit)
    w_gate = columns(mlp_gate.T, hidw)
    w_up = columns(mlp_up.T, hidw)
    w_down = columns(mlp_down, hidw)

    def adapter(sections, cot, pre_gain, cod_gain, w_state, w_inject):
        prelude, lower, upper, top = (sections[at].astype(F32) for at in range(4))
        cot_f = cot[...].astype(F32)
        cut = (tp_count, rows, unit)
        left = jnp.concatenate([upper.reshape(cut), lower.reshape(cut)], axis=1)
        left = left.reshape(2 * block, unit).astype(BF)
        states = dot(left, w_state[...]).reshape(tp_count, 2 * rows, wide)
        prior = dot((prelude * pre_gain[...]).astype(BF), w_inject[...]).reshape(tp_count, rows, wide)
        row_sums = [
            jnp.sum(prelude * prelude, axis=-1, keepdims=True),
            jnp.sum(top * top, axis=-1, keepdims=True),
            jnp.sum(cot_f * cod_gain[...] * top, axis=-1, keepdims=True),
        ]
        sums = put_parts(jnp.zeros((block, unit), F32), 0, row_sums)
        coda = cod_gain[...]
        high = rounded(coda)
        at = lax.broadcasted_iota(jnp.int32, (rows, unit), 0)
        gains = jnp.where(at == 0, high, jnp.where(at == 1, coda - high, 0.0))
        gains = jnp.broadcast_to(gains[None], cut)
        extra = jnp.concatenate(
            [top.reshape(cut), cot_f.reshape(cut), gains, sums.reshape(cut)], axis=-1
        )
        return (jnp.concatenate([states, prior, extra], axis=1),)

    (sent,) = fused(
        adapter,
        [((tp_count, 4 * rows, wide), BF)],
        sections,
        cot,
        pre_gain,
        cod_gain,
        w_state,
        w_inject,
    )
    arrived = exchange(sent, "tensor")

    arrived, w_gate, w_up, w_down = lax.optimization_barrier((arrived, w_gate, w_up, w_down))

    def blocks_of(value):
        return jnp.concatenate(
            [value[None, :, at * unit : (at + 1) * unit] for at in range(group)], axis=0
        )

    def mix(dp, arrived, gain):
        sums = jnp.sum(arrived[...].astype(F32), axis=0)
        totals = sums[3 * rows :, 3 * unit :]
        near = [arrived[dp * group + at].astype(F32)[3 * rows :] for at in range(group)]
        top = jnp.concatenate([value[:, :unit] for value in near], axis=-1)
        cot_f = jnp.concatenate([value[:, unit : 2 * unit] for value in near], axis=-1)
        coda = jnp.concatenate(
            [value[0:1, 2 * unit : 3 * unit] + value[1:2, 2 * unit : 3 * unit] for value in near], axis=-1
        )
        pre_scale = lax.rsqrt(pick_whole(totals, 0) / D + EPSILON)
        top_scale = lax.rsqrt(pick_whole(totals, 2) / D + EPSILON)
        inner = pick_whole(totals, 4) / D
        prior = sums[2 * rows : 3 * rows]
        mixed_u = rounded(sums[:rows] + pre_scale * prior)
        mixed_l = rounded(sums[rows : 2 * rows] + pre_scale * prior)
        cot_u = rounded(
            top_scale * (cot_f * coda) - top * (top_scale * top_scale * top_scale) * inner
        )
        own = jnp.concatenate(
            [put_parts(mixed_u, part, [pre_scale, top_scale]), mixed_l, cot_u], axis=0
        )
        spread = jnp.broadcast_to(own[None], (tp_count,) + own.shape)
        ready = jnp.concatenate([mixed_u, mixed_l], axis=0) * gain[...]
        kept = jnp.concatenate([mixed_u, mixed_l, cot_u, prior], axis=0)
        return spread, kept, blocks_of(ready)

    eight = ((rows, wide), F32)
    sent, kept_8, ready_8 = fused(
        mix,
        [((tp_count, 3 * rows, wide), BF), ((4 * rows, wide), F32), ((group, 2 * rows, unit), BF)],
        dp_s,
        arrived,
        gain,
    )

    def from_segments(values):
        return [lax.dynamic_index_in_dim(values, seg_index, 0, keepdims=False)] + [
            rotate(
                lax.dynamic_index_in_dim(values, (seg_index + step) % seg_count, 0, keepdims=False), step
            )
            for step in range(1, seg_count)
        ]

    ready_8 = jnp.concatenate(
        from_segments(ready_8) + [jnp.zeros((4 * rows, unit), BF)], axis=0
    )
    arrived = exchange(sent, "tensor")
    arrived, ready_8 = lax.optimization_barrier((arrived, ready_8))

    def forward_upper(core, arrived, gain, w_gate, w_up, w_down):
        mixed = arrived[:, :rows, :].astype(F32).reshape(block, wide)
        cot_u = arrived[...].astype(F32)[:, 2 * rows :].reshape(block, wide).astype(BF)
        factor = gain[...]
        squares = jnp.sum(jnp.where(factor > 0.0, mixed * mixed, 0.0), axis=-1, keepdims=True)
        ready = (mixed * factor).astype(BF)
        sums = jnp.concatenate(
            [
                put_parts(dot_t(ready, w_gate[...]), hid, [squares]),
                dot_t(ready, w_up[...]),
                dot_t(cot_u, w_down[...]),
            ],
            axis=-1,
        )
        return halves(sums, core)

    def forward_lower(core, arrived, gain, w_gate, w_up):
        every = arrived[...].astype(F32)
        mixed_u = every[:, :rows].reshape(block, wide)
        mixed = every[:, rows : 2 * rows].reshape(block, wide)
        cot_u = every[:, 2 * rows :].reshape(block, wide)
        factor = gain[...]
        squares = jnp.sum(jnp.where(factor > 0.0, mixed * mixed, 0.0), axis=-1, keepdims=True)
        ready = (mixed * factor).astype(BF)
        sums = jnp.concatenate(
            [put_parts(dot_t(ready, w_gate[...]), hid, [squares]), dot_t(ready, w_up[...])], axis=-1
        )
        mine, other = halves(sums, core)
        scales = mixed_u[:, :unit]
        at = lanes((block, 128))
        scales = jnp.where(at == 0, pick_whole(scales, part), pick_whole(scales, part + 2))
        return mine, other, cot_u, scales

    three_half = [((half, 3 * hidw), F32), ((half, 3 * hidw), BF)]
    two_half = [((half, 2 * hidw), F32), ((half, 2 * hidw), BF)]
    mine, other = fused(forward_upper, three_half, core_s, arrived, gain, w_gate, w_up, w_down)

    def add_squares(mine, other):
        total = mine[...] + other[...].astype(F32)
        first = total[:, :hidw]
        first = put_parts(first, hid, [pick_whole(first, hid)])
        total = jnp.concatenate([first, total[:, hidw:]], axis=-1)
        return total, total

    mine, other = fused(add_squares, three_half, mine, core_swap(other))
    landed = chip_swap(other)
    arrived, landed = lax.optimization_barrier((arrived, landed))
    mine_l, other_l, cot_u, norm_scales = fused(
        forward_lower,
        two_half + [((block, wide), BF), ((block, 128), F32)],
        core_s,
        arrived,
        gain,
        w_gate,
        w_up,
    )

    def own_quarter(values, chip):
        return jnp.where(chip == 0, values[:quarter], values[quarter:])

    def sigmoid(value):
        return 1.0 / (1.0 + jnp.exp(-value))

    def activate(chip, mine, landed):
        total = mine[...] + landed[...].astype(F32)
        kinds = [total[:, at * hidw : (at + 1) * hidw] for at in range(3)]
        scale = lax.rsqrt(pick_whole(kinds[0], hid) / D + EPSILON)
        gate = jnp.where(lanes(kinds[0].shape) < hid, kinds[0] * scale, 0.0)
        up_value = kinds[1] * scale
        sig = sigmoid(gate)
        act = gate * sig
        g_gate = rounded(kinds[2] * up_value * sig * (1.0 + gate * (1.0 - sig)))
        g_up = rounded(kinds[2] * act)
        inner = jnp.sum(g_gate * gate + g_up * up_value, axis=-1, keepdims=True)
        pair = jnp.concatenate([put_parts(g_gate, hid, [inner, scale]), g_up], axis=-1)
        scaled = jnp.concatenate([g_gate, g_up], axis=-1) * scale
        return pair, act * up_value, own_quarter(scaled, chip)

    pair, hidden_u, quarter_u = fused(
        activate,
        [((half, 2 * hidw), BF), ((half, hidw), BF), ((quarter, 2 * hidw), BF)],
        chip_s,
        mine,
        landed,
    )

    def activate_lower(mine, landed, hidden_u):
        total = mine[...] + landed[...].astype(F32)
        gate, up_value = total[:, :hidw], total[:, hidw:]
        scale = lax.rsqrt(pick_whole(gate, hid) / D + EPSILON)
        gate = jnp.where(lanes(gate.shape) < hid, gate * scale, 0.0)
        up_value = up_value * scale
        sig = sigmoid(gate)
        act = gate * sig
        slope = up_value * sig * (1.0 + gate * (1.0 - sig))
        hidden = jnp.concatenate([hidden_u[...].astype(F32), act * up_value], axis=-1)
        scales = jnp.broadcast_to(scale, (half, 128))
        return jnp.concatenate([gate, up_value, act, slope], axis=-1), scales, hidden

    def all_quarters(values):
        return lax.all_gather(values, ("segment", "dp"), axis=0, tiled=False)

    def normed_sums(core, mine, other, w_gate, w_up):
        both = joined(mine[...].astype(F32), other[...].astype(F32), core)
        g_gate, g_up = both[:, :hidw], both[:, hidw:]
        sums = dot(g_gate.astype(BF), w_gate[...]) + dot(g_up.astype(BF), w_up[...])
        sums = put_parts(sums, part, [pick_whole(g_gate, hid)])
        at = lanes((block, 128))
        scales = jnp.where(at >= 0, pick_whole(g_gate, hid + 2), 0.0)
        return sums.reshape(tp_count, rows, wide), scales

    normed_outs = [((tp_count, rows, wide), BF), ((block, 128), F32)]
    def quarter_inputs(dp, quarter_u, sections, norm_scales, pre_gain):
        begin = dp * quarter
        mine = [sections[kind, pl.ds(begin, quarter), :].astype(F32) for kind in range(3)]
        scale = pick(norm_scales[pl.ds(begin, quarter), :], 0)
        inject = mine[0] * scale * pre_gain[...]
        kinds = [quarter_u[...].astype(F32), mine[2], mine[1], inject]
        return (jnp.concatenate(kinds, axis=-1),)

    (upper,) = fused(
        quarter_inputs,
        [((quarter, 2 * hidw + 3 * unit), BF)],
        dp_s,
        quarter_u,
        sections,
        norm_scales,
        pre_gain,
    )
    sent, scales = fused(normed_sums, normed_outs, core_s, pair, core_swap(pair), w_gate, w_up)
    arrived = exchange(sent, "tensor")
    arrived, upper, ready_8 = lax.optimization_barrier((arrived, upper, ready_8))
    upper = all_quarters(upper)
    shared = lax.all_gather(ready_8, "tensor", axis=0, tiled=False)

    def mixed_back(tp, arrived, cot, mixed, scales, gain):
        sums = jnp.sum(arrived[...].astype(F32), axis=0)
        scale = pick(scales[pl.ds(tp * rows, rows), :], 0)
        inner = pick_whole(sums[:, :unit], part) / scale / D
        factor = gain[...]
        weighted = sums * factor
        g_mixed = rounded(
            cot + scale * weighted - mixed * (scale * scale * scale) * inner
        )
        gain_part = jnp.sum(jnp.where(factor > 0.0, sums * mixed * scale, 0.0), axis=0, keepdims=True)
        return g_mixed, gain_part

    def upper_back(tp, arrived, kept_8, scales, gain):
        mixed, cot = kept_8[0:rows, :], kept_8[2 * rows : 3 * rows, :]
        g_mixed, gain_part = mixed_back(tp, arrived, cot, mixed, scales, gain)
        spread = jnp.broadcast_to(g_mixed[None], (tp_count, rows, wide))
        gain_part = jnp.broadcast_to(gain_part, (rows, wide))
        return spread, jnp.concatenate([g_mixed, gain_part], axis=0)

    mine_l, other_l = fused(add_squares, two_half, mine_l, core_swap(other_l))
    landed_l = chip_swap(other_l)
    lower, half_scales, hidden = fused(
        activate_lower,
        [((half, 4 * hidw), F32), ((half, 128), F32), ((half, 2 * hidw), BF)],
        mine_l,
        landed_l,
        hidden_u,
    )
    hidden_other = core_swap(hidden)
    spread_shape = ((tp_count, rows, wide), BF)
    sent, upper_8 = fused(
        upper_back,
        [spread_shape, ((2 * rows, wide), F32)],
        tp_s,
        arrived,
        kept_8,
        scales,
        gain,
    )
    arrived_u = exchange(sent, "tensor")

    def state_back(tp, arrived, w_state):
        g_mixed = arrived[...].astype(F32).reshape(block, wide).astype(BF)
        g_state = dot_t(g_mixed, w_state[...]).reshape(tp_count, 1, rows, unit)
        at = lax.broadcasted_iota(jnp.int32, (tp_count, dp_count, rows, unit), 1)
        return (
            jnp.where(at == tp // group, g_state, 0.0).reshape(tp_count * dp_count, rows, unit),
        )

    (sent,) = fused(
        state_back, [((tp_count * dp_count, rows, unit), BF)], tp_s, arrived_u, w_state
    )
    sent, other_l = lax.optimization_barrier((sent, other_l))
    arrived = exchange(sent, ("tensor", "dp"))

    def lower_cot(dp, arrived):
        blocks = []
        for at in range(group):
            first = (dp * group + at) * dp_count
            blocks.append(sum(arrived[first + one].astype(F32) for one in range(dp_count)))
        cot = rounded(jnp.concatenate(blocks, axis=-1))
        return jnp.broadcast_to(cot[None], (tp_count, rows, wide)), cot

    sent, cot_l8 = fused(lower_cot, [spread_shape, eight], dp_s, arrived)
    sent, lower, hidden_other = lax.optimization_barrier((sent, lower, hidden_other))
    arrived_c = exchange(sent, "tensor")

    def hidden_back(core, arrived, w_down):
        cot = arrived[...].astype(F32).reshape(block, wide).astype(BF)
        return halves(dot_t(cot, w_down[...]), core)

    one_half = [((half, hidw), F32), ((half, hidw), BF)]
    mine, other = fused(hidden_back, one_half, core_s, arrived_c, w_down)

    def add(mine, other):
        total = mine[...] + other[...].astype(F32)
        return total, total

    mine, other = fused(add, one_half, mine, core_swap(other))
    landed = chip_swap(other)

    def lower_hidden(chip, mine, landed, lower, scales):
        g_hidden = mine[...] + landed[...].astype(F32)
        gate, up_value, act, slope = (lower[:, at * hidw : (at + 1) * hidw] for at in range(4))
        g_gate = rounded(g_hidden * slope)
        g_up = rounded(g_hidden * act)
        inner = jnp.sum(g_gate * gate + g_up * up_value, axis=-1, keepdims=True)
        scale = pick(scales[...], 0)
        pair = jnp.concatenate([put_parts(g_gate, hid, [inner, scale]), g_up], axis=-1)
        scaled = jnp.concatenate([g_gate, g_up], axis=-1) * scale
        return pair, own_quarter(scaled, chip)

    pair, quarter_l = fused(
        lower_hidden,
        [((half, 2 * hidw), BF), ((quarter, 2 * hidw), BF)],
        chip_s,
        mine,
        landed,
        lower,
        half_scales,
    )
    sent, scales = fused(normed_sums, normed_outs, core_s, pair, core_swap(pair), w_gate, w_up)

    def down_part(core, mine, other, cot_u, arrived_c):
        hidden = joined(mine[...].astype(F32), other[...].astype(F32), core)
        first, second = hidden[:, :hidw].T.astype(BF), hidden[:, hidw:].T.astype(BF)
        cot_l = arrived_c[...].astype(F32).reshape(block, wide).astype(BF)
        blocks = []
        for at in range(group):
            cut = slice(at * unit, (at + 1) * unit)
            total = dot(first, cot_u[:, cut]) + dot(second, cot_l[:, cut])
            blocks.append(total[:hid, :part][None])
        return (jnp.concatenate(blocks, axis=0),)

    sent, hidden, hidden_other = lax.optimization_barrier((sent, hidden, hidden_other))
    (down,) = fused(
        down_part, [((group, hid, part), BF)], core_s, hidden, hidden_other, cot_u, arrived_c
    )
    down = lax.psum_scatter(down, "segment", scatter_dimension=0, tiled=True)
    arrived = exchange(sent, "tensor")

    def two_rows(value, count):
        high = rounded(value)
        at = lax.broadcasted_iota(jnp.int32, (count, value.shape[1]), 0)
        return jnp.where(at == 0, high, jnp.where(at == 1, value - high, 0.0))

    def lower_back(tp, arrived, cot_8, kept_8, scales, gain, upper_8):
        mixed, prior = kept_8[rows : 2 * rows, :], kept_8[3 * rows :, :]
        g_mixed, gain_part = mixed_back(tp, arrived, cot_8[...], mixed, scales, gain)
        inner = jnp.sum((upper_8[0:rows, :] + g_mixed) * prior, axis=-1, keepdims=True)
        total = upper_8[rows : rows + 1, :] + gain_part
        own = jnp.concatenate([put_parts(g_mixed, part, [inner]), two_rows(total, rows)], axis=0)
        both = jnp.concatenate([upper_8[0:rows, :], g_mixed], axis=0)
        return jnp.broadcast_to(own[None], (tp_count, 2 * rows, wide)), blocks_of(both)

    sent, g_mixed_8 = fused(
        lower_back,
        [((tp_count, 2 * rows, wide), BF), ((group, 2 * rows, unit), BF)],
        tp_s,
        arrived,
        cot_l8,
        kept_8,
        scales,
        gain,
        upper_8,
    )
    g_mixed_8 = jnp.concatenate(from_segments(g_mixed_8), axis=0)
    sent, upper = lax.optimization_barrier((sent, upper))
    arrived = exchange(sent, "tensor")
    arrived, g_mixed_8 = lax.optimization_barrier((arrived, g_mixed_8))
    lower_shared = exchange(jnp.broadcast_to(g_mixed_8[None], (tp_count,) + g_mixed_8.shape), "tensor")

    def inject_back(core, arrived, arrived_u, w_inject, gain, sections, norm_scales):
        every = arrived[...].astype(F32)
        lower_f = every[:, :rows].reshape(block, wide)
        inner = pick_whole(lower_f[:, :unit], part)
        g_mixed_l = jnp.where(gain[...] > 0.0, lower_f, 0.0).astype(BF)
        g_mixed_u = arrived_u[...].astype(F32).reshape(block, wide).astype(BF)
        sums = dot_t(g_mixed_u, w_inject[...]) + dot_t(g_mixed_l, w_inject[...])
        mine, other = halves(put_parts(sums, part, [inner]), core)
        prelude = sections[0].astype(F32)
        gain_row = jnp.sum(sums * prelude * pick(norm_scales[...], 0), axis=0, keepdims=True)
        mine = jnp.concatenate([mine, two_rows(gain_row, 16)], axis=0)
        other = jnp.concatenate([other, two_rows(gain_row, 16)], axis=0)
        gains = jnp.sum(every[:, rows:], axis=0)
        gains = gains[0:1] + gains[1:2]
        return mine, other, blocks_of(two_rows(gains, 16))

    more = half + 16
    one_part = [((more, unit), F32), ((more, unit), BF)]
    mine, other, last = fused(
        inject_back,
        one_part + [((group, 16, unit), BF)],
        core_s,
        arrived,
        arrived_u,
        w_inject,
        gain,
        sections,
        norm_scales,
    )

    def add_inner(mine, other):
        total = mine[...] + other[...].astype(F32)
        sums = put_parts(total[:half], part, [pick_whole(total[:half], part)])
        gain_row = total[half : half + 1] + total[half + 1 : half + 2]
        total = jnp.concatenate([sums, two_rows(gain_row, 16)], axis=0)
        return total, total

    mine, other = fused(add_inner, one_part, mine, core_swap(other))
    landed = chip_swap(other)

    def prelude_back(core, chip, mine, landed, sections, norm_scales, pre_gain, cot, last):
        total = mine[...] + landed[...].astype(F32)
        gain_row = total[half : half + 1] + total[half + 1 : half + 2]
        total = total[:half]
        inner = pick_whole(total, part) / D
        prelude, _ = halves(sections[0].astype(F32), core)
        scale, _ = halves(norm_scales[...], core)
        scale = pick(scale, 0)
        scaled = total * pre_gain[...]
        grad = scale * scaled - prelude * (scale * scale * scale) * inner
        top_scale = pick(norm_scales[...], 1)
        coda_row = jnp.sum(
            cot[...].astype(F32) * sections[3].astype(F32) * top_scale, axis=0, keepdims=True
        )
        own = jnp.concatenate(
            [own_quarter(grad, chip), two_rows(gain_row, 8), two_rows(coda_row, 8)], axis=0
        ).astype(BF)
        own = jnp.broadcast_to(own[None], (group,) + own.shape)
        return (jnp.concatenate([last[...], own], axis=1),)

    (last,) = fused(
        prelude_back,
        [((group, 32 + quarter, unit), BF)],
        core_s,
        chip_s,
        mine,
        landed,
        sections,
        norm_scales,
        pre_gain,
        cot,
        last,
    )
    last, lower_shared = lax.optimization_barrier((last, lower_shared))
    last = exchange(last, "segment")

    lower_all = all_quarters(quarter_l)

    def hidden_grads(seg, shared, upper, lower):
        total = 0.0
        every = shared[...].astype(F32)
        for step in range(seg_count):
            begin = lax.rem(seg + seg_count - step, seg_count) * dp_count
            for number, source in enumerate((upper, lower)):
                first = (2 * step + number) * rows
                left = every[:, first : first + rows].reshape(block, unit).T.astype(BF)
                right = source[pl.ds(begin, dp_count), :, : 2 * hidw].astype(F32)
                total = total + dot(left, right.reshape(block, 2 * hidw).astype(BF))
        return total[:part, :hid], total[:part, hidw : hidw + hid]

    seg_s = seg_index.reshape(1)
    grad_gate, grad_up = fused(
        hidden_grads, [((part, hid), BF), ((part, hid), BF)], seg_s, shared, upper, lower_all
    )

    def adapter_grads(seg, upper, lower_shared):
        g_state, g_inject = 0.0, 0.0
        every = lower_shared[...].astype(F32)
        for step in range(seg_count):
            begin = lax.rem(seg + seg_count - step, seg_count) * dp_count
            first = 2 * step * rows
            right_u = every[:, first : first + rows].reshape(block, unit).astype(BF)
            right_l = every[:, first + rows : first + 2 * rows].reshape(block, unit).astype(BF)
            kinds = [
                turned(
                    upper[pl.ds(begin, dp_count), :, first : first + unit]
                    .astype(F32)
                    .reshape(block, unit)
                )
                for first in range(2 * hidw, 2 * hidw + 3 * unit, unit)
            ]
            g_state = g_state + dot(kinds[0], right_u) + dot(kinds[1], right_l)
            g_inject = g_inject + dot(kinds[2], right_u) + dot(kinds[2], right_l)
        return g_state[:part, :part], g_inject[:part, :part]

    grad_state, grad_inject = fused(
        adapter_grads,
        [((part, part), BF), ((part, part), BF)],
        seg_s,
        upper,
        lower_shared,
    )

    def finish(last):
        tail = sum(last[at].astype(F32) for at in range(seg_count))
        begin = 16 + quarter
        gains = [tail[row : row + 1] + tail[row + 1 : row + 2] for row in (0, begin, begin + 8)]
        prelude = [last[at].astype(F32)[16 : 16 + quarter] for at in range(seg_count)]
        prelude = turned(jnp.concatenate(prelude, axis=0))[:part]
        return *gains, prelude

    row = ((1, unit), F32)
    mlp_row, prelude_row, coda_row, out_prelude = fused(
        finish, [row, row, row, ((part, block), BF)], last
    )
    return (
        out_prelude.T,
        prelude_row[0, :part],
        coda_row[0, :part],
        grad_state,
        grad_inject,
        grad_gate,
        grad_up,
        down[0],
        mlp_row[0, :part].astype(BF),
    )


def solution(mesh):
    placed = (
        P("segment", "dp", "tensor"),
        P("dp", "tensor"),
        P("tensor"),
        P("tensor"),
        P("dp"),
        P("tensor", "dp"),
        P("tensor", "dp"),
        P("dp", "tensor"),
        P("dp", "tensor"),
        P("tensor", "dp"),
    )
    return jax.shard_map(
        local,
        mesh=mesh,
        in_specs=placed,
        out_specs=(
            P("dp", "tensor"),
            P("tensor"),
            P("tensor"),
            P("tensor", ("dp", "segment")),
            P("tensor", ("dp", "segment")),
            P(("dp", "segment"), "tensor"),
            P(("dp", "segment"), "tensor"),
            P("tensor", ("dp", "segment")),
            P(("dp", "segment")),
        ),
        check_vma=False,
    )
```

```python
import jax
import jax.numpy as jnp
from jax import lax
from jax.experimental import pallas as pl
from jax.experimental.pallas import tpu as pltpu
from jax.sharding import PartitionSpec as P

D = 5280
EPSILON = 1e-06
BF = jnp.bfloat16
F32 = jnp.float32
LIMIT = 40 * 1024 * 1024


def up(value):
    return -(-value // 128) * 128


def dot(left, right):
    return jnp.dot(left, right, preferred_element_type=F32)


def dot_t(left, right):
    return lax.dot_general(left, right, (((1,), (1,)), ((), ())), preferred_element_type=F32)


def turned(value):
    return value.astype(F32).T.astype(BF)


def rounded(value):
    return value.astype(BF).astype(F32)


def lanes(shape):
    return lax.broadcasted_iota(jnp.int32, shape, len(shape) - 1)


def pick(value, lane):
    return jnp.sum(jnp.where(lanes(value.shape) == lane, value, 0.0), axis=-1, keepdims=True)


def pick_whole(value, lane):
    at = lanes(value.shape)
    return jnp.sum(jnp.where((at == lane) | (at == lane + 1), value, 0.0), axis=-1, keepdims=True)


def put_parts(value, lane, scalars):
    at = lanes(value.shape)
    for number, scalar in enumerate(scalars):
        high = rounded(scalar)
        value = jnp.where(at == lane + 2 * number, high, value)
        value = jnp.where(at == lane + 2 * number + 1, scalar - high, value)
    return value


def fused(body, outs, *args):
    scalar = [arg.dtype == jnp.int32 for arg in args]

    def kernel(*refs):
        given = [ref[0] if is_scalar else ref for ref, is_scalar in zip(refs, scalar)]
        results = body(*given)
        for ref, value in zip(refs[len(args) :], results):
            if value is not None:
                if value.shape == ref.shape:
                    ref[...] = value.astype(ref.dtype)
                else:
                    ref[...] = jnp.zeros(ref.shape, ref.dtype)
                    ref[tuple(slice(0, size) for size in value.shape)] = value.astype(ref.dtype)

    specs = [
        pl.BlockSpec(memory_space=pltpu.SMEM if is_scalar else pltpu.VMEM) for is_scalar in scalar
    ]
    return pl.pallas_call(
        kernel,
        out_shape=[jax.ShapeDtypeStruct(shape, kind) for shape, kind in outs],
        in_specs=specs,
        out_specs=[pl.BlockSpec(memory_space=pltpu.VMEM) for _ in outs],
        compiler_params=pltpu.CompilerParams(vmem_limit_bytes=LIMIT),
    )(*args)


def exchange(values, axis):
    return lax.all_to_all(values, axis, 0, 0, tiled=True)


def core_swap(values):
    return lax.ppermute(values, "dp", [(0, 1), (1, 0), (2, 3), (3, 2)])


def chip_swap(values):
    return lax.ppermute(values, "dp", [(0, 2), (2, 0), (1, 3), (3, 1)])


def rotate(values, step):
    return lax.ppermute(values, "segment", [(at, (at + step) % 4) for at in range(4)])


def halves(values, core):
    count, width = values.shape
    blocks = values.reshape(2, 2, count // 4, width)
    first, second = blocks[:, 0].reshape(count // 2, width), blocks[:, 1].reshape(count // 2, width)
    return jnp.where(core == 0, first, second), jnp.where(core == 0, second, first)


def joined(mine, other, core):
    count, width = mine.shape
    first = jnp.where(core == 0, mine, other).reshape(2, 1, count // 2, width)
    second = jnp.where(core == 0, other, mine).reshape(2, 1, count // 2, width)
    return jnp.concatenate([first, second], axis=1).reshape(2 * count, width)


def gathered_blocks(values, core, chip):
    other = core_swap(values)
    two = jnp.stack([jnp.where(core == 0, values, other), jnp.where(core == 0, other, values)])
    far = chip_swap(two)
    four = jnp.stack([jnp.where(chip == 0, two, far), jnp.where(chip == 0, far, two)])
    return four.reshape((4 * values.shape[0],) + values.shape[1:])


def local(
    checkpoints,
    cot_out,
    prelude_gain,
    coda_gain,
    mlp_gain,
    adapt_state,
    adapt_inject,
    mlp_gate,
    mlp_up,
    mlp_down,
):
    dp_count = lax.axis_size("dp")
    seg_count = lax.axis_size("segment")
    tp_count = lax.axis_size("tensor")
    dp_index = lax.axis_index("dp").astype(jnp.int32)
    seg_index = lax.axis_index("segment").astype(jnp.int32)
    tp_index = lax.axis_index("tensor").astype(jnp.int32)
    core = dp_index % 2
    chip = dp_index // 2
    block = checkpoints.shape[1]
    quarter = block // seg_count
    half = 2 * quarter
    part = checkpoints.shape[2]
    unit = up(part + 8)
    hid = mlp_gate.shape[1]
    hidw = up(hid + 8)
    group = mlp_gain.shape[0] // part
    wide = group * unit
    rows = block // tp_count
    core_s, chip_s, dp_s, tp_s = (x.reshape(1) for x in (core, chip, dp_index, tp_index))

    def padded(values, axis, width):
        return jnp.pad(
            values,
            [(0, width - size) if at == axis else (0, 0) for at, size in enumerate(values.shape)],
        )

    def grouped(values, axis):
        shape = values.shape[:axis] + (group, part) + values.shape[axis + 1 :]
        values = padded(values.reshape(shape), axis + 1, unit)
        return values.reshape(shape[:axis] + (wide,) + shape[axis + 2 :])

    chunks = padded(checkpoints[0], 1, unit).reshape(seg_count, 1, quarter, unit)
    chunks = jnp.broadcast_to(chunks, (seg_count, dp_count, quarter, unit))
    sections = exchange(
        chunks.reshape(seg_count * dp_count, quarter, unit), ("segment", "dp")
    ).reshape(4, block, unit)
    cot_own = lax.dynamic_slice_in_dim(cot_out, seg_index * quarter, quarter, 0)
    cot = gathered_blocks(padded(cot_own, 1, unit), core, chip)
    pre_gain = padded(prelude_gain[None], 1, unit)
    cod_gain = padded(coda_gain[None], 1, unit)
    gain = grouped(mlp_gain[None], 1)

    def by_columns(weight):
        count, width = weight.shape
        blocks = []
        for at in range(group):
            row = lax.broadcasted_iota(jnp.int32, (width, unit), 0)
            col = lax.broadcasted_iota(jnp.int32, (width, unit), 1)
            chosen = jnp.where((row == col + at * part) & (col < part), 1.0, 0.0).astype(BF)
            blocks.append(dot(weight[...], chosen))
        return (jnp.concatenate(blocks, axis=-1),)

    def columns(weight, count):
        return fused(by_columns, [((count, wide), BF)], weight)[0]

    w_state = columns(adapt_state, unit)
    w_inject = columns(adapt_inject, unit)
    w_gate = columns(mlp_gate.T, hidw)
    w_up = columns(mlp_up.T, hidw)
    w_down = columns(mlp_down, hidw)

    def adapter(sections, cot, pre_gain, cod_gain, w_state, w_inject):
        prelude, lower, upper, top = (sections[at].astype(F32) for at in range(4))
        cot_f = cot[...].astype(F32)
        cut = (tp_count, rows, unit)
        left = jnp.concatenate([upper.reshape(cut), lower.reshape(cut)], axis=1)
        left = left.reshape(2 * block, unit).astype(BF)
        states = dot(left, w_state[...]).reshape(tp_count, 2 * rows, wide)
        prior = dot((prelude * pre_gain[...]).astype(BF), w_inject[...]).reshape(tp_count, rows, wide)
        row_sums = [
            jnp.sum(prelude * prelude, axis=-1, keepdims=True),
            jnp.sum(top * top, axis=-1, keepdims=True),
            jnp.sum(cot_f * cod_gain[...] * top, axis=-1, keepdims=True),
        ]
        sums = put_parts(jnp.zeros((block, unit), F32), 0, row_sums)
        coda = cod_gain[...]
        high = rounded(coda)
        at = lax.broadcasted_iota(jnp.int32, (rows, unit), 0)
        gains = jnp.where(at == 0, high, jnp.where(at == 1, coda - high, 0.0))
        gains = jnp.broadcast_to(gains[None], cut)
        extra = jnp.concatenate(
            [top.reshape(cut), cot_f.reshape(cut), gains, sums.reshape(cut)], axis=-1
        )
        return (jnp.concatenate([states, prior, extra], axis=1),)

    (sent,) = fused(
        adapter,
        [((tp_count, 4 * rows, wide), BF)],
        sections,
        cot,
        pre_gain,
        cod_gain,
        w_state,
        w_inject,
    )
    arrived = exchange(sent, "tensor")

    arrived, w_gate, w_up, w_down = lax.optimization_barrier((arrived, w_gate, w_up, w_down))

    def blocks_of(value):
        return jnp.concatenate(
            [value[None, :, at * unit : (at + 1) * unit] for at in range(group)], axis=0
        )

    def mix(dp, arrived, gain):
        sums = jnp.sum(arrived[...].astype(F32), axis=0)
        totals = sums[3 * rows :, 3 * unit :]
        near = [arrived[dp * group + at].astype(F32)[3 * rows :] for at in range(group)]
        top = jnp.concatenate([value[:, :unit] for value in near], axis=-1)
        cot_f = jnp.concatenate([value[:, unit : 2 * unit] for value in near], axis=-1)
        coda = jnp.concatenate(
            [value[0:1, 2 * unit : 3 * unit] + value[1:2, 2 * unit : 3 * unit] for value in near], axis=-1
        )
        pre_scale = lax.rsqrt(pick_whole(totals, 0) / D + EPSILON)
        top_scale = lax.rsqrt(pick_whole(totals, 2) / D + EPSILON)
        inner = pick_whole(totals, 4) / D
        prior = sums[2 * rows : 3 * rows]
        mixed_u = rounded(sums[:rows] + pre_scale * prior)
        mixed_l = rounded(sums[rows : 2 * rows] + pre_scale * prior)
        cot_u = rounded(
            top_scale * (cot_f * coda) - top * (top_scale * top_scale * top_scale) * inner
        )
        own = jnp.concatenate(
            [put_parts(mixed_u, part, [pre_scale, top_scale]), mixed_l, cot_u], axis=0
        )
        spread = jnp.broadcast_to(own[None], (tp_count,) + own.shape)
        ready = jnp.concatenate([mixed_u, mixed_l], axis=0) * gain[...]
        kept = jnp.concatenate([mixed_u, mixed_l, cot_u, prior], axis=0)
        return spread, kept, blocks_of(ready)

    eight = ((rows, wide), F32)
    sent, kept_8, ready_8 = fused(
        mix,
        [((tp_count, 3 * rows, wide), BF), ((4 * rows, wide), F32), ((group, 2 * rows, unit), BF)],
        dp_s,
        arrived,
        gain,
    )

    def from_segments(values):
        return [lax.dynamic_index_in_dim(values, seg_index, 0, keepdims=False)] + [
            rotate(
                lax.dynamic_index_in_dim(values, (seg_index + step) % seg_count, 0, keepdims=False), step
            )
            for step in range(1, seg_count)
        ]

    ready_8 = jnp.concatenate(
        from_segments(ready_8) + [jnp.zeros((4 * rows, unit), BF)], axis=0
    )
    arrived = exchange(sent, "tensor")
    arrived, ready_8 = lax.optimization_barrier((arrived, ready_8))

    def forward_upper(core, arrived, gain, w_gate, w_up, w_down):
        mixed = arrived[:, :rows, :].astype(F32).reshape(block, wide)
        cot_u = arrived[...].astype(F32)[:, 2 * rows :].reshape(block, wide).astype(BF)
        factor = gain[...]
        squares = jnp.sum(jnp.where(factor > 0.0, mixed * mixed, 0.0), axis=-1, keepdims=True)
        ready = (mixed * factor).astype(BF)
        sums = jnp.concatenate(
            [
                put_parts(dot_t(ready, w_gate[...]), hid, [squares]),
                dot_t(ready, w_up[...]),
                dot_t(cot_u, w_down[...]),
            ],
            axis=-1,
        )
        return halves(sums, core)

    def forward_lower(core, arrived, gain, w_gate, w_up):
        every = arrived[...].astype(F32)
        mixed_u = every[:, :rows].reshape(block, wide)
        mixed = every[:, rows : 2 * rows].reshape(block, wide)
        cot_u = every[:, 2 * rows :].reshape(block, wide)
        factor = gain[...]
        squares = jnp.sum(jnp.where(factor > 0.0, mixed * mixed, 0.0), axis=-1, keepdims=True)
        ready = (mixed * factor).astype(BF)
        sums = jnp.concatenate(
            [put_parts(dot_t(ready, w_gate[...]), hid, [squares]), dot_t(ready, w_up[...])], axis=-1
        )
        mine, other = halves(sums, core)
        scales = mixed_u[:, :unit]
        at = lanes((block, 128))
        scales = jnp.where(at == 0, pick_whole(scales, part), pick_whole(scales, part + 2))
        return mine, other, cot_u, scales

    three_half = [((half, 3 * hidw), F32), ((half, 3 * hidw), BF)]
    two_half = [((half, 2 * hidw), F32), ((half, 2 * hidw), BF)]
    mine, other = fused(forward_upper, three_half, core_s, arrived, gain, w_gate, w_up, w_down)

    def add_squares(mine, other):
        total = mine[...] + other[...].astype(F32)
        first = total[:, :hidw]
        first = put_parts(first, hid, [pick_whole(first, hid)])
        total = jnp.concatenate([first, total[:, hidw:]], axis=-1)
        return total, total

    mine, other = fused(add_squares, three_half, mine, core_swap(other))
    landed = chip_swap(other)
    arrived, landed = lax.optimization_barrier((arrived, landed))
    mine_l, other_l, cot_u, norm_scales = fused(
        forward_lower,
        two_half + [((block, wide), BF), ((block, 128), F32)],
        core_s,
        arrived,
        gain,
        w_gate,
        w_up,
    )

    def own_quarter(values, chip):
        return jnp.where(chip == 0, values[:quarter], values[quarter:])

    def sigmoid(value):
        return 1.0 / (1.0 + jnp.exp(-value))

    def activate(chip, mine, landed):
        total = mine[...] + landed[...].astype(F32)
        kinds = [total[:, at * hidw : (at + 1) * hidw] for at in range(3)]
        scale = lax.rsqrt(pick_whole(kinds[0], hid) / D + EPSILON)
        gate = jnp.where(lanes(kinds[0].shape) < hid, kinds[0] * scale, 0.0)
        up_value = kinds[1] * scale
        sig = sigmoid(gate)
        act = gate * sig
        g_gate = rounded(kinds[2] * up_value * sig * (1.0 + gate * (1.0 - sig)))
        g_up = rounded(kinds[2] * act)
        inner = jnp.sum(g_gate * gate + g_up * up_value, axis=-1, keepdims=True)
        pair = jnp.concatenate([put_parts(g_gate, hid, [inner, scale]), g_up], axis=-1)
        scaled = jnp.concatenate([g_gate, g_up], axis=-1) * scale
        return pair, act * up_value, own_quarter(scaled, chip)

    pair, hidden_u, quarter_u = fused(
        activate,
        [((half, 2 * hidw), BF), ((half, hidw), BF), ((quarter, 2 * hidw), BF)],
        chip_s,
        mine,
        landed,
    )

    def activate_lower(mine, landed, hidden_u):
        total = mine[...] + landed[...].astype(F32)
        gate, up_value = total[:, :hidw], total[:, hidw:]
        scale = lax.rsqrt(pick_whole(gate, hid) / D + EPSILON)
        gate = jnp.where(lanes(gate.shape) < hid, gate * scale, 0.0)
        up_value = up_value * scale
        sig = sigmoid(gate)
        act = gate * sig
        slope = up_value * sig * (1.0 + gate * (1.0 - sig))
        hidden = jnp.concatenate([hidden_u[...].astype(F32), act * up_value], axis=-1)
        scales = jnp.broadcast_to(scale, (half, 128))
        return jnp.concatenate([gate, up_value, act, slope], axis=-1), scales, hidden

    def all_quarters(values):
        return lax.all_gather(values, ("segment", "dp"), axis=0, tiled=False)

    def normed_sums(core, mine, other, w_gate, w_up):
        both = joined(mine[...].astype(F32), other[...].astype(F32), core)
        g_gate, g_up = both[:, :hidw], both[:, hidw:]
        sums = dot(g_gate.astype(BF), w_gate[...]) + dot(g_up.astype(BF), w_up[...])
        sums = put_parts(sums, part, [pick_whole(g_gate, hid)])
        at = lanes((block, 128))
        scales = jnp.where(at >= 0, pick_whole(g_gate, hid + 2), 0.0)
        return sums.reshape(tp_count, rows, wide), scales

    normed_outs = [((tp_count, rows, wide), BF), ((block, 128), F32)]
    def quarter_inputs(dp, quarter_u, sections, norm_scales, pre_gain):
        begin = dp * quarter
        mine = [sections[kind, pl.ds(begin, quarter), :].astype(F32) for kind in range(3)]
        scale = pick(norm_scales[pl.ds(begin, quarter), :], 0)
        inject = mine[0] * scale * pre_gain[...]
        kinds = [quarter_u[...].astype(F32), mine[2], mine[1], inject]
        return (jnp.concatenate(kinds, axis=-1),)

    (upper,) = fused(
        quarter_inputs,
        [((quarter, 2 * hidw + 3 * unit), BF)],
        dp_s,
        quarter_u,
        sections,
        norm_scales,
        pre_gain,
    )
    sent, scales = fused(normed_sums, normed_outs, core_s, pair, core_swap(pair), w_gate, w_up)
    arrived = exchange(sent, "tensor")
    arrived, upper, ready_8 = lax.optimization_barrier((arrived, upper, ready_8))
    upper = all_quarters(upper)
    shared = lax.all_gather(ready_8, "tensor", axis=0, tiled=False)

    def mixed_back(tp, arrived, cot, mixed, scales, gain):
        sums = jnp.sum(arrived[...].astype(F32), axis=0)
        scale = pick(scales[pl.ds(tp * rows, rows), :], 0)
        inner = pick_whole(sums[:, :unit], part) / scale / D
        factor = gain[...]
        weighted = sums * factor
        g_mixed = rounded(
            cot + scale * weighted - mixed * (scale * scale * scale) * inner
        )
        gain_part = jnp.sum(jnp.where(factor > 0.0, sums * mixed * scale, 0.0), axis=0, keepdims=True)
        return g_mixed, gain_part

    def upper_back(tp, arrived, kept_8, scales, gain):
        mixed, cot = kept_8[0:rows, :], kept_8[2 * rows : 3 * rows, :]
        g_mixed, gain_part = mixed_back(tp, arrived, cot, mixed, scales, gain)
        spread = jnp.broadcast_to(g_mixed[None], (tp_count, rows, wide))
        gain_part = jnp.broadcast_to(gain_part, (rows, wide))
        return spread, jnp.concatenate([g_mixed, gain_part], axis=0)

    mine_l, other_l = fused(add_squares, two_half, mine_l, core_swap(other_l))
    landed_l = chip_swap(other_l)
    lower, half_scales, hidden = fused(
        activate_lower,
        [((half, 4 * hidw), F32), ((half, 128), F32), ((half, 2 * hidw), BF)],
        mine_l,
        landed_l,
        hidden_u,
    )
    hidden_other = core_swap(hidden)
    spread_shape = ((tp_count, rows, wide), BF)
    sent, upper_8 = fused(
        upper_back,
        [spread_shape, ((2 * rows, wide), F32)],
        tp_s,
        arrived,
        kept_8,
        scales,
        gain,
    )
    arrived_u = exchange(sent, "tensor")

    def state_back(tp, arrived, w_state):
        g_mixed = arrived[...].astype(F32).reshape(block, wide).astype(BF)
        g_state = dot_t(g_mixed, w_state[...]).reshape(tp_count, 1, rows, unit)
        at = lax.broadcasted_iota(jnp.int32, (tp_count, dp_count, rows, unit), 1)
        return (
            jnp.where(at == tp // group, g_state, 0.0).reshape(tp_count * dp_count, rows, unit),
        )

    (sent,) = fused(
        state_back, [((tp_count * dp_count, rows, unit), BF)], tp_s, arrived_u, w_state
    )
    sent, other_l = lax.optimization_barrier((sent, other_l))
    arrived = exchange(sent, ("tensor", "dp"))

    def lower_cot(dp, arrived):
        blocks = []
        for at in range(group):
            first = (dp * group + at) * dp_count
            blocks.append(sum(arrived[first + one].astype(F32) for one in range(dp_count)))
        cot = rounded(jnp.concatenate(blocks, axis=-1))
        return jnp.broadcast_to(cot[None], (tp_count, rows, wide)), cot

    sent, cot_l8 = fused(lower_cot, [spread_shape, eight], dp_s, arrived)
    sent, lower, hidden_other = lax.optimization_barrier((sent, lower, hidden_other))
    arrived_c = exchange(sent, "tensor")

    def hidden_back(core, arrived, w_down):
        cot = arrived[...].astype(F32).reshape(block, wide).astype(BF)
        return halves(dot_t(cot, w_down[...]), core)

    one_half = [((half, hidw), F32), ((half, hidw), BF)]
    mine, other = fused(hidden_back, one_half, core_s, arrived_c, w_down)

    def add(mine, other):
        total = mine[...] + other[...].astype(F32)
        return total, total

    mine, other = fused(add, one_half, mine, core_swap(other))
    landed = chip_swap(other)

    def lower_hidden(chip, mine, landed, lower, scales):
        g_hidden = mine[...] + landed[...].astype(F32)
        gate, up_value, act, slope = (lower[:, at * hidw : (at + 1) * hidw] for at in range(4))
        g_gate = rounded(g_hidden * slope)
        g_up = rounded(g_hidden * act)
        inner = jnp.sum(g_gate * gate + g_up * up_value, axis=-1, keepdims=True)
        scale = pick(scales[...], 0)
        pair = jnp.concatenate([put_parts(g_gate, hid, [inner, scale]), g_up], axis=-1)
        scaled = jnp.concatenate([g_gate, g_up], axis=-1) * scale
        return pair, own_quarter(scaled, chip)

    pair, quarter_l = fused(
        lower_hidden,
        [((half, 2 * hidw), BF), ((quarter, 2 * hidw), BF)],
        chip_s,
        mine,
        landed,
        lower,
        half_scales,
    )
    sent, scales = fused(normed_sums, normed_outs, core_s, pair, core_swap(pair), w_gate, w_up)

    def down_part(core, mine, other, cot_u, arrived_c):
        hidden = joined(mine[...].astype(F32), other[...].astype(F32), core)
        first, second = hidden[:, :hidw].T.astype(BF), hidden[:, hidw:].T.astype(BF)
        cot_l = arrived_c[...].astype(F32).reshape(block, wide).astype(BF)
        blocks = []
        for at in range(group):
            cut = slice(at * unit, (at + 1) * unit)
            total = dot(first, cot_u[:, cut]) + dot(second, cot_l[:, cut])
            blocks.append(total[:hid, :part][None])
        return (jnp.concatenate(blocks, axis=0),)

    sent, hidden, hidden_other = lax.optimization_barrier((sent, hidden, hidden_other))
    (down,) = fused(
        down_part, [((group, hid, part), BF)], core_s, hidden, hidden_other, cot_u, arrived_c
    )
    down = lax.psum_scatter(down, "segment", scatter_dimension=0, tiled=True)
    arrived = exchange(sent, "tensor")

    def two_rows(value, count):
        high = rounded(value)
        at = lax.broadcasted_iota(jnp.int32, (count, value.shape[1]), 0)
        return jnp.where(at == 0, high, jnp.where(at == 1, value - high, 0.0))

    def lower_back(tp, arrived, cot_8, kept_8, scales, gain, upper_8):
        mixed, prior = kept_8[rows : 2 * rows, :], kept_8[3 * rows :, :]
        g_mixed, gain_part = mixed_back(tp, arrived, cot_8[...], mixed, scales, gain)
        inner = jnp.sum((upper_8[0:rows, :] + g_mixed) * prior, axis=-1, keepdims=True)
        total = upper_8[rows : rows + 1, :] + gain_part
        own = jnp.concatenate([put_parts(g_mixed, part, [inner]), two_rows(total, rows)], axis=0)
        both = jnp.concatenate([upper_8[0:rows, :], g_mixed], axis=0)
        return jnp.broadcast_to(own[None], (tp_count, 2 * rows, wide)), blocks_of(both)

    sent, g_mixed_8 = fused(
        lower_back,
        [((tp_count, 2 * rows, wide), BF), ((group, 2 * rows, unit), BF)],
        tp_s,
        arrived,
        cot_l8,
        kept_8,
        scales,
        gain,
        upper_8,
    )
    g_mixed_8 = jnp.concatenate(from_segments(g_mixed_8), axis=0)
    sent, upper = lax.optimization_barrier((sent, upper))
    arrived = exchange(sent, "tensor")
    arrived, g_mixed_8 = lax.optimization_barrier((arrived, g_mixed_8))
    lower_shared = exchange(jnp.broadcast_to(g_mixed_8[None], (tp_count,) + g_mixed_8.shape), "tensor")

    def inject_back(core, arrived, arrived_u, w_inject, gain, sections, norm_scales):
        every = arrived[...].astype(F32)
        lower_f = every[:, :rows].reshape(block, wide)
        inner = pick_whole(lower_f[:, :unit], part)
        g_mixed_l = jnp.where(gain[...] > 0.0, lower_f, 0.0).astype(BF)
        g_mixed_u = arrived_u[...].astype(F32).reshape(block, wide).astype(BF)
        sums = dot_t(g_mixed_u, w_inject[...]) + dot_t(g_mixed_l, w_inject[...])
        mine, other = halves(put_parts(sums, part, [inner]), core)
        prelude = sections[0].astype(F32)
        gain_row = jnp.sum(sums * prelude * pick(norm_scales[...], 0), axis=0, keepdims=True)
        mine = jnp.concatenate([mine, two_rows(gain_row, 16)], axis=0)
        other = jnp.concatenate([other, two_rows(gain_row, 16)], axis=0)
        gains = jnp.sum(every[:, rows:], axis=0)
        gains = gains[0:1] + gains[1:2]
        return mine, other, blocks_of(two_rows(gains, 16))

    more = half + 16
    one_part = [((more, unit), F32), ((more, unit), BF)]
    mine, other, last = fused(
        inject_back,
        one_part + [((group, 16, unit), BF)],
        core_s,
        arrived,
        arrived_u,
        w_inject,
        gain,
        sections,
        norm_scales,
    )

    def add_inner(mine, other):
        total = mine[...] + other[...].astype(F32)
        sums = put_parts(total[:half], part, [pick_whole(total[:half], part)])
        gain_row = total[half : half + 1] + total[half + 1 : half + 2]
        total = jnp.concatenate([sums, two_rows(gain_row, 16)], axis=0)
        return total, total

    mine, other = fused(add_inner, one_part, mine, core_swap(other))
    landed = chip_swap(other)

    def prelude_back(core, chip, mine, landed, sections, norm_scales, pre_gain, cot, last):
        total = mine[...] + landed[...].astype(F32)
        gain_row = total[half : half + 1] + total[half + 1 : half + 2]
        total = total[:half]
        inner = pick_whole(total, part) / D
        prelude, _ = halves(sections[0].astype(F32), core)
        scale, _ = halves(norm_scales[...], core)
        scale = pick(scale, 0)
        scaled = total * pre_gain[...]
        grad = scale * scaled - prelude * (scale * scale * scale) * inner
        top_scale = pick(norm_scales[...], 1)
        coda_row = jnp.sum(
            cot[...].astype(F32) * sections[3].astype(F32) * top_scale, axis=0, keepdims=True
        )
        own = jnp.concatenate(
            [own_quarter(grad, chip), two_rows(gain_row, 8), two_rows(coda_row, 8)], axis=0
        ).astype(BF)
        own = jnp.broadcast_to(own[None], (group,) + own.shape)
        return (jnp.concatenate([last[...], own], axis=1),)

    (last,) = fused(
        prelude_back,
        [((group, 32 + quarter, unit), BF)],
        core_s,
        chip_s,
        mine,
        landed,
        sections,
        norm_scales,
        pre_gain,
        cot,
        last,
    )
    last, lower_shared = lax.optimization_barrier((last, lower_shared))
    last = exchange(last, "segment")

    lower_all = all_quarters(quarter_l)

    def hidden_grads(seg, shared, upper, lower):
        total = 0.0
        every = shared[...].astype(F32)
        for step in range(seg_count):
            begin = lax.rem(seg + seg_count - step, seg_count) * dp_count
            for number, source in enumerate((upper, lower)):
                first = (2 * step + number) * rows
                left = every[:, first : first + rows].reshape(block, unit).T.astype(BF)
                right = source[pl.ds(begin, dp_count), :, : 2 * hidw].astype(F32)
                total = total + dot(left, right.reshape(block, 2 * hidw).astype(BF))
        return total[:part, :hid], total[:part, hidw : hidw + hid]

    seg_s = seg_index.reshape(1)
    grad_gate, grad_up = fused(
        hidden_grads, [((part, hid), BF), ((part, hid), BF)], seg_s, shared, upper, lower_all
    )

    def adapter_grads(seg, upper, lower_shared):
        g_state, g_inject = 0.0, 0.0
        every = lower_shared[...].astype(F32)
        for step in range(seg_count):
            begin = lax.rem(seg + seg_count - step, seg_count) * dp_count
            first = 2 * step * rows
            right_u = every[:, first : first + rows].reshape(block, unit).astype(BF)
            right_l = every[:, first + rows : first + 2 * rows].reshape(block, unit).astype(BF)
            kinds = [
                turned(
                    upper[pl.ds(begin, dp_count), :, first : first + unit]
                    .astype(F32)
                    .reshape(block, unit)
                )
                for first in range(2 * hidw, 2 * hidw + 3 * unit, unit)
            ]
            g_state = g_state + dot(kinds[0], right_u) + dot(kinds[1], right_l)
            g_inject = g_inject + dot(kinds[2], right_u) + dot(kinds[2], right_l)
        return g_state[:part, :part], g_inject[:part, :part]

    grad_state, grad_inject = fused(
        adapter_grads,
        [((part, part), BF), ((part, part), BF)],
        seg_s,
        upper,
        lower_shared,
    )

    def finish(last):
        tail = sum(last[at].astype(F32) for at in range(seg_count))
        begin = 16 + quarter
        gains = [tail[row : row + 1] + tail[row + 1 : row + 2] for row in (0, begin, begin + 8)]
        prelude = [last[at].astype(F32)[16 : 16 + quarter] for at in range(seg_count)]
        prelude = turned(jnp.concatenate(prelude, axis=0))[:part]
        return *gains, prelude

    row = ((1, unit), F32)
    mlp_row, prelude_row, coda_row, out_prelude = fused(
        finish, [row, row, row, ((part, block), BF)], last
    )
    return (
        out_prelude.T,
        prelude_row[0, :part],
        coda_row[0, :part],
        grad_state,
        grad_inject,
        grad_gate,
        grad_up,
        down[0],
        mlp_row[0, :part].astype(BF),
    )


def solution(mesh):
    placed = (
        P("segment", "dp", "tensor"),
        P("dp", "tensor"),
        P("tensor"),
        P("tensor"),
        P("dp"),
        P("tensor", "dp"),
        P("tensor", "dp"),
        P("dp", "tensor"),
        P("dp", "tensor"),
        P("tensor", "dp"),
    )
    return jax.shard_map(
        local,
        mesh=mesh,
        in_specs=placed,
        out_specs=(
            P("dp", "tensor"),
            P("tensor"),
            P("tensor"),
            P("tensor", ("dp", "segment")),
            P("tensor", ("dp", "segment")),
            P(("dp", "segment"), "tensor"),
            P(("dp", "segment"), "tensor"),
            P("tensor", ("dp", "segment")),
            P(("dp", "segment")),
        ),
        check_vma=False,
    )
```
